128 devices in a mesh: dp: 8 (over y, x_hi), seq: 16 (over x_lo, z, core).
Axes of the slice: x: 4 (x_hi: 2, x_lo: 2; x = x_hi * 2 + x_lo), y: 4, z: 4, core: 2. Of those that a mesh axis runs over, the one named last changes fastest.
Arguments:
- queries: bfloat16 [8, 16, 256, 40, 128], P('dp', 'seq'), may hold values from -6 to 6
- key_proj: bfloat16 [8, 16, 256, 40, 128], P('dp', 'seq'), may hold values from -6 to 6
- value_proj: bfloat16 [8, 16, 256, 40, 128], P('dp', 'seq'), may hold values from -6 to 6
- out_grad: bfloat16 [8, 16, 256, 40, 128], P('dp', 'seq'), may hold values from -6 to 6
- query_gain: float32 [40, 128], P('dp'), may hold values from 0.5 to 5
- key_gain: float32 [40, 128], P('dp'), may hold values from 0.5 to 5
Outputs:
- query_grad: bfloat16 [8, 16, 256, 40, 128], P('dp', 'seq')
- key_grad: bfloat16 [8, 16, 256, 40, 128], P('dp', 'seq')
- value_grad: bfloat16 [8, 16, 256, 40, 128], P('dp', 'seq')
- query_gain_grad: float32 [40, 128], P('dp')
- key_gain_grad: float32 [40, 128], P('dp')
The draws below stay inside these ranges and needn't reach their ends.
All inputs are finite; a program needn't handle non-finite values.
Results may differ from the reference program's by a relative error of at most 0.0034.
The reference program's roundings to bfloat16 on the way count: a program that leaves them out, or rounds other values in their place, can miss the bound.
Values may be sent and summed in bfloat16 or wider, within the bound.
A program may use at most 128 MiB of HBM per device.

```python
import math
import jax
import jax.numpy as jnp
from jax import lax

HEADS = 40
HDIM = 128
PATCHES = 256
FRAMES = 16
EPIS = 8


def gain_base(key):
    return jnp.exp(jax.random.uniform(key, (HEADS, HDIM), jnp.float32, math.log(0.5), math.log(2.0)))


def draw_query_gain(key, part):
    key = jax.random.fold_in(key, 11)
    values = gain_base(key)
    return values


def draw_key_gain(key, part):
    key = jax.random.fold_in(key, 12)
    values = gain_base(key)
    return values


def draw_queries(key, part):
    key = jax.random.fold_in(key, 21)
    values = jnp.clip(jax.random.normal(key, (EPIS, FRAMES, PATCHES, HEADS, HDIM), jnp.float32), -6.0, 6.0)
    return values.astype(jnp.bfloat16)


def draw_key_proj(key, part):
    key = jax.random.fold_in(key, 22)
    values = jnp.clip(jax.random.normal(key, (EPIS, FRAMES, PATCHES, HEADS, HDIM), jnp.float32), -6.0, 6.0)
    return values.astype(jnp.bfloat16)


def level_of(rng, extent, cuts, smallest, top_value):
    def one(position, blocks):
        steps = jax.random.uniform(jax.random.fold_in(jax.random.fold_in(rng, 6), position), (blocks,), jnp.float32, smallest / len(cuts), top_value / len(cuts))
        return jnp.repeat(jnp.exp(steps), extent[position] // blocks).reshape((-1,) + (1,) * (len(extent) - position - 1))

    level = one(*cuts[0])
    for cut in cuts[1:]:
        level = level * one(*cut)
    return level


def bell_draw(key, shape, scale, bound, split=(), held_as=jnp.bfloat16):
    values = jax.random.normal(key, shape, jnp.float32) * scale
    if len(split) > 0:
        values = level_of(key, shape, split, -0.22, 0.18) * values
    return jnp.clip(values, min=-bound, max=bound).astype(held_as)


def setup_inputs(seed: int = 0) -> dict:
    streams_of = jax.random.split(jax.random.key(seed), 7)
    queries = draw_queries(jax.random.fold_in(streams_of[6], 71), 0)
    key_proj = draw_key_proj(jax.random.fold_in(streams_of[6], 71), 0)
    value_proj = bell_draw(streams_of[2], (EPIS, FRAMES, PATCHES, HEADS, HDIM), 1.0, 6.0, ((0, 8), (1, 16)))
    out_grad = bell_draw(streams_of[3], (EPIS, FRAMES, PATCHES, HEADS, HDIM), 1.0, 6.0, ((0, 8), (1, 16)))
    query_gain = draw_query_gain(jax.random.fold_in(streams_of[6], 71), 0)
    key_gain = draw_key_gain(jax.random.fold_in(streams_of[6], 71), 0)
    return dict(queries=queries, key_proj=key_proj, value_proj=value_proj, out_grad=out_grad, query_gain=query_gain, key_gain=key_gain)


EPSILON = 1e-06

def widen(values):
    return lax.optimization_barrier(values).astype(jnp.float32)

def normalize(values):
    wide = values.astype(jnp.float32)
    inverse = lax.rsqrt(lax.optimization_barrier(jnp.mean(wide * wide, axis=-1, keepdims=True)) + EPSILON)
    return (wide * inverse, inverse)

def norm_back(step, hat, inverse, gain):
    step_wide = widen(step)
    gained = gain * step_wide
    result = (inverse * (gained - hat * lax.optimization_barrier(jnp.mean(gained * hat, axis=-1, keepdims=True)))).astype(jnp.bfloat16)
    gain_part = lax.optimization_barrier(jnp.sum(step_wide * hat, axis=tuple(range(step.ndim - 2))))
    return (result, gain_part)

def attention_grads(query_norm, key_norm, value_in, grad_in):
    highest = lax.Precision.HIGHEST
    frames = query_norm.shape[0]
    scaling = 1.0 / math.sqrt(query_norm.shape[-1])
    query_wide = widen(query_norm)
    key_wide = widen(key_norm)
    value_wide = widen(value_in)
    grad_wide = widen(grad_in)
    scores = jnp.einsum('fphd,gphd->phfg', query_wide, key_wide, precision=highest) * scaling
    row_ids = lax.broadcasted_iota(jnp.int32, (frames, frames), 0)
    col_ids = lax.broadcasted_iota(jnp.int32, (frames, frames), 1)
    allowed = col_ids <= row_ids
    scores = jnp.where(allowed, scores, -jnp.inf)
    largest = lax.optimization_barrier(jnp.max(scores, axis=-1, keepdims=True))
    expo = jnp.exp(scores - largest)
    probability = expo / lax.optimization_barrier(jnp.sum(expo, axis=-1, keepdims=True))
    prob_wide = widen(probability.astype(jnp.bfloat16))
    attn_out = jnp.einsum('phfg,gphd->fphd', prob_wide, value_wide, precision=highest)
    row_dots = jnp.transpose(lax.optimization_barrier(jnp.sum(grad_wide * attn_out, axis=-1)), (1, 2, 0))
    prob_grad = jnp.einsum('fphd,gphd->phfg', grad_wide, value_wide, precision=highest)
    score_grad = probability * (prob_grad - row_dots[..., None])
    score_wide = widen(score_grad.astype(jnp.bfloat16))
    query_step = (jnp.einsum('phfg,gphd->fphd', score_wide, key_wide, precision=highest) * scaling).astype(jnp.bfloat16)
    key_step = (jnp.einsum('phfg,fphd->gphd', score_wide, query_wide, precision=highest) * scaling).astype(jnp.bfloat16)
    value_step = jnp.einsum('phfg,fphd->gphd', prob_wide, grad_wide, precision=highest).astype(jnp.bfloat16)
    return (query_step, key_step, value_step)

def reference(queries, key_proj, value_proj, out_grad, query_gain, key_gain):

    def episode(pieces):
        query_in, key_in, value_in, grad_in = pieces
        query_hat, query_inverse = normalize(query_in)
        key_hat, key_inverse = normalize(key_in)
        query_norm = (query_hat * query_gain).astype(jnp.bfloat16)
        key_norm = (key_hat * key_gain).astype(jnp.bfloat16)
        query_step, key_step, value_step = attention_grads(query_norm, key_norm, value_in, grad_in)
        query_out, query_part = norm_back(query_step, query_hat, query_inverse, query_gain)
        key_out, key_part = norm_back(key_step, key_hat, key_inverse, key_gain)
        return (query_out, key_out, value_step, query_part, key_part)
    query_out, key_out, value_out, query_parts, key_parts = lax.map(episode, (queries, key_proj, value_proj, out_grad))
    return (query_out, key_out, value_out, lax.optimization_barrier(jnp.sum(query_parts, axis=0)), lax.optimization_barrier(jnp.sum(key_parts, axis=0)))
```

```python
import functools
import math

import jax
import jax.numpy as jnp
from jax import lax
from jax.experimental import pallas as pl
from jax.experimental.pallas import tpu as pltpu
from jax.sharding import PartitionSpec as P

EPSILON = 1e-06
HEADS = 40
HDIM = 128
SEQ = 16
CHUNKS = 4
GROUP = 16
MESH = pl.DeviceIdType.MESH
NEGATIVE = -1e30


def peer_of(me, step):
    x = lax.rem(lax.div(me, 8) + lax.div(step, 8), 2)
    z = lax.rem(lax.div(me, 2) + lax.div(step, 2), 4)
    core = lax.rem(me + step, 2)
    return x * 8 + z * 2 + core


def kernel(
    dp_size,
    q_hbm, k_hbm, v_hbm, g_hbm, qgain_ref, kgain_ref,
    oq, ok, ov, oqg, okg,
    raw, nrm, rcv, stg, ret, mask, gsend, gbuf, gain, acc, rsend, rbuf, asend, abuf,
    raw_sem, fwd_send, fwd_recv, ret_send, ret_recv, val_send, val_recv, out_sem,
    gain_send, gain_recv, rs_send, rs_recv, ag_send, ag_recv,
):
    me = lax.axis_index("seq")
    dp = lax.axis_index("dp")
    rows = q_hbm.shape[1]
    part = rows // CHUNKS
    local_heads = HEADS // dp_size
    pad = gsend.shape[0] // 2
    scaling = 1.0 / math.sqrt(HDIM)

    def remote(src, dst, send, recv, seq):
        return pltpu.make_async_remote_copy(
            src_ref=src, dst_ref=dst, send_sem=send, recv_sem=recv,
            device_id={"seq": seq}, device_id_type=MESH,
        )

    def remote_dp(src, dst, send, recv, other):
        return pltpu.make_async_remote_copy(
            src_ref=src, dst_ref=dst, send_sem=send, recv_sem=recv,
            device_id={"dp": other}, device_id_type=MESH,
        )

    for a, source in enumerate((q_hbm, k_hbm)):
        pltpu.make_async_copy(source, raw.at[a], raw_sem.at[a]).start()
    gsend[...] = jnp.zeros_like(gsend)
    gsend[0:local_heads] = qgain_ref[...]
    gsend[pad : pad + local_heads] = kgain_ref[...]

    barrier = pltpu.get_barrier_semaphore()
    for step in range(1, SEQ):
        pl.semaphore_signal(
            barrier, inc=1, device_id={"seq": lax.rem(me + step, SEQ)}, device_id_type=MESH
        )
    for step in range(1, dp_size):
        pl.semaphore_signal(
            barrier, inc=1, device_id={"dp": lax.rem(dp + step, dp_size)}, device_id_type=MESH
        )
    pl.semaphore_wait(barrier, SEQ - 1 + dp_size - 1)

    for step in range(1, dp_size):
        remote_dp(
            gsend, gbuf.at[dp], gain_send, gain_recv, lax.rem(dp + step, dp_size)
        ).start()
    pltpu.make_async_copy(gsend, gbuf.at[dp], gain_recv).start()

    def send_values(c):
        here = pl.ds(c * part, part)

        def one(step, carry):
            seq = peer_of(me, step)
            for a, source in ((2, v_hbm), (3, g_hbm)):
                remote(
                    source.at[seq, here], rcv.at[a, c, me], fwd_send.at[a], fwd_recv.at[a, c], seq
                ).start()
            return carry

        lax.fori_loop(1, SEQ, one, 0)
        for a, source in ((2, v_hbm), (3, g_hbm)):
            pltpu.make_async_copy(source.at[me, here], rcv.at[a, c, me], fwd_recv.at[a, c]).start()

    def normalized(a, seq, here):
        wide = raw[a, seq, here].astype(jnp.float32)
        inverse = lax.rsqrt(jnp.mean(wide * wide, axis=-1, keepdims=True) + EPSILON)
        return wide * inverse, inverse

    def by_head(tile, factor):
        split = tile.reshape(part // HEADS, HEADS, HDIM)
        return (split * factor[None]).reshape(part, HDIM)

    def send_normalized(c):
        here = pl.ds(c * part, part)

        def one(step, carry):
            seq = peer_of(me, step)
            for a in range(2):
                hat, _ = normalized(a, seq, here)
                nrm[a, seq, here] = by_head(hat, gain[a]).astype(jnp.bfloat16)

            @pl.when(step > 0)
            def _():
                for a in range(2):
                    remote(
                        nrm.at[a, seq, here], rcv.at[a, c, me],
                        fwd_send.at[a], fwd_recv.at[a, c], seq,
                    ).start()

            @pl.when(step == 0)
            def _():
                for a in range(2):
                    pltpu.make_async_copy(
                        nrm.at[a, me, here], rcv.at[a, c, me], fwd_recv.at[a, c]
                    ).start()

            return carry

        lax.fori_loop(0, SEQ, one, 0)

    send_values(0)
    row_ids = lax.broadcasted_iota(jnp.int32, mask.shape, 0)
    col_ids = lax.broadcasted_iota(jnp.int32, mask.shape, 1)
    allowed = (lax.rem(row_ids, GROUP) == lax.rem(col_ids, GROUP)) & (col_ids <= row_ids)
    mask[...] = jnp.where(allowed, 0.0, NEGATIVE)
    acc[...] = jnp.zeros_like(acc)

    pltpu.make_async_copy(gbuf, gbuf, gain_recv).wait()
    for d in range(dp_size):
        for a in range(2):
            gain[a, d * local_heads : (d + 1) * local_heads] = gbuf[
                d, a * pad : a * pad + local_heads
            ]
    for a, source in enumerate((q_hbm, k_hbm)):
        pltpu.make_async_copy(source, raw.at[a], raw_sem.at[a]).wait()

    send_normalized(0)
    for c in range(1, CHUNKS):
        send_values(c)
        send_normalized(c)

    def contract(left, right, dims):
        return lax.dot_general(left, right, (dims, ((), ())), preferred_element_type=jnp.float32)

    def attention(c):
        for a in range(4):
            pltpu.make_async_copy(rcv.at[a, c], rcv.at[a, c], fwd_recv.at[a, c]).wait()

        def block(b, carry):
            here = pl.ds(pl.multiple_of(b * GROUP, GROUP), GROUP)
            wide = SEQ * GROUP
            query, key, value, grad = (
                rcv[a, c, :, here, :].reshape(wide, HDIM) for a in range(4)
            )
            scores = contract(query, key, ((1,), (1,))) * scaling + mask[...]
            expo = jnp.exp(scores - jnp.max(scores, axis=-1, keepdims=True))
            probability = expo / jnp.sum(expo, axis=-1, keepdims=True)
            prob_low = probability.astype(jnp.bfloat16)
            prob_grad = contract(grad, value, ((1,), (1,)))
            row_dots = jnp.sum(prob_low.astype(jnp.float32) * prob_grad, axis=-1, keepdims=True)
            score_low = (probability * (prob_grad - row_dots)).astype(jnp.bfloat16)
            results = (
                contract(score_low, key, ((1,), (0,))) * scaling,
                contract(score_low, query, ((0,), (0,))) * scaling,
                contract(prob_low, grad, ((0,), (0,))),
            )
            for a, result in enumerate(results):
                stg[a, c, :, here, :] = result.astype(jnp.bfloat16).reshape(SEQ, GROUP, HDIM)
            return carry

        lax.fori_loop(0, part // GROUP, block, 0)

    def send_steps(c):
        def one(step, carry):
            seq = peer_of(me, step)
            for a in range(2):
                remote(
                    stg.at[a, c, seq], ret.at[a, c, me], ret_send.at[a], ret_recv.at[a, c], seq
                ).start()
            return carry

        lax.fori_loop(1, SEQ, one, 0)
        for a in range(2):
            pltpu.make_async_copy(stg.at[a, c, me], ret.at[a, c, me], ret_recv.at[a, c]).start()

    def send_value_grads(c):
        here = pl.ds(c * part, part)

        def one(step, carry):
            seq = peer_of(me, step)
            remote(stg.at[2, c, seq], ov.at[me, here], val_send, val_recv, seq).start()
            return carry

        lax.fori_loop(1, SEQ, one, 0)
        pltpu.make_async_copy(stg.at[2, c, me], ov.at[me, here], val_recv).start()

    def norm_back(c):
        here = pl.ds(c * part, part)
        for a in range(2):
            pltpu.make_async_copy(ret.at[a, c], ret.at[a, c], ret_recv.at[a, c]).wait()

        def one(seq, carry):
            for a in range(2):
                hat, inverse = normalized(a, seq, here)
                step = ret[a, c, seq].astype(jnp.float32)
                gained = by_head(step, gain[a])
                mean = jnp.mean(gained * hat, axis=-1, keepdims=True)
                raw[a, seq, here] = (inverse * (gained - hat * mean)).astype(jnp.bfloat16)
                acc[a] += jnp.sum((step * hat).reshape(part // HEADS, HEADS, HDIM), axis=0)
            return carry

        lax.fori_loop(0, SEQ, one, 0)
        for a, out in enumerate((oq, ok)):
            pltpu.make_async_copy(raw.at[a, :, here], out.at[:, here], out_sem.at[a]).start()

    for c in range(CHUNKS):
        attention(c)
        send_steps(c)
    for c in range(CHUNKS):
        send_value_grads(c)
    for c in range(CHUNKS):
        norm_back(c)

    rsend[...] = jnp.zeros_like(rsend)
    for d in range(dp_size):
        for a in range(2):
            rsend[d, a * pad : a * pad + local_heads] = acc[
                a, d * local_heads : (d + 1) * local_heads
            ]
    for step in range(1, dp_size):
        other = lax.rem(dp + step, dp_size)
        remote_dp(rsend.at[other], rbuf.at[dp], rs_send, rs_recv, other).start()
    pltpu.make_async_copy(rsend.at[dp], rbuf.at[dp], rs_recv).start()
    pltpu.make_async_copy(rbuf, rbuf, rs_recv).wait()
    asend[...] = jnp.sum(rbuf[...], axis=0)
    for step in range(1, SEQ):
        seq = lax.rem(me + step, SEQ)
        remote(asend, abuf.at[me], ag_send, ag_recv, seq).start()
    pltpu.make_async_copy(asend, abuf.at[me], ag_recv).start()
    pltpu.make_async_copy(abuf, abuf, ag_recv).wait()
    total = jnp.sum(abuf[...], axis=0)
    oqg[...] = total[0:local_heads]
    okg[...] = total[pad : pad + local_heads]

    others = pl.ds(0, SEQ - 1)
    pltpu.make_async_copy(ov, ov, val_recv).wait()
    for a, out in enumerate((oq, ok)):
        pltpu.make_async_copy(out, out, out_sem.at[a]).wait()
    for a in range(4):
        pltpu.make_async_copy(oq.at[others], oq.at[others], fwd_send.at[a]).wait()
    for a in range(2):
        pltpu.make_async_copy(oq.at[others], oq.at[others], ret_send.at[a]).wait()
    pltpu.make_async_copy(oq.at[others], oq.at[others], val_send).wait()
    if dp_size > 1:
        most = pl.ds(0, dp_size - 1)
        pltpu.make_async_copy(gbuf.at[most], gbuf.at[most], gain_send).wait()
        pltpu.make_async_copy(rbuf.at[most], rbuf.at[most], rs_send).wait()
    pltpu.make_async_copy(abuf.at[others], abuf.at[others], ag_send).wait()


def body(dp_size, queries, key_proj, value_proj, out_grad, query_gain, key_gain):
    shape = queries.shape
    rows = shape[2] * HEADS // SEQ
    part = rows // CHUNKS
    local_heads = query_gain.shape[0]
    pad = -(-local_heads // 8) * 8
    flat = [v.reshape(SEQ, rows, HDIM) for v in (queries, key_proj, value_proj, out_grad)]
    low, wide = jnp.bfloat16, jnp.float32
    anywhere = pl.BlockSpec(memory_space=pl.ANY)
    vmem = pl.BlockSpec(memory_space=pltpu.VMEM)
    dma = pltpu.SemaphoreType.DMA
    big = jax.ShapeDtypeStruct((SEQ, rows, HDIM), low)
    small = jax.ShapeDtypeStruct((local_heads, HDIM), wide)
    query_grad, key_grad, value_grad, query_total, key_total = pl.pallas_call(
        functools.partial(kernel, dp_size),
        out_shape=(big, big, big, small, small),
        in_specs=[anywhere] * 4 + [vmem] * 2,
        out_specs=(anywhere, anywhere, anywhere, vmem, vmem),
        scratch_shapes=[
            pltpu.VMEM((2, SEQ, rows, HDIM), low),
            pltpu.VMEM((2, SEQ, rows, HDIM), low),
            pltpu.VMEM((4, CHUNKS, SEQ, part, HDIM), low),
            pltpu.VMEM((3, CHUNKS, SEQ, part, HDIM), low),
            pltpu.VMEM((2, CHUNKS, SEQ, part, HDIM), low),
            pltpu.VMEM((SEQ * GROUP, SEQ * GROUP), wide),
            pltpu.VMEM((2 * pad, HDIM), wide),
            pltpu.VMEM((dp_size, 2 * pad, HDIM), wide),
            pltpu.VMEM((2, HEADS, HDIM), wide),
            pltpu.VMEM((2, HEADS, HDIM), wide),
            pltpu.VMEM((dp_size, 2 * pad, HDIM), wide),
            pltpu.VMEM((dp_size, 2 * pad, HDIM), wide),
            pltpu.VMEM((2 * pad, HDIM), wide),
            pltpu.VMEM((SEQ, 2 * pad, HDIM), wide),
            dma((2,)),
            dma((4,)),
            dma((4, CHUNKS)),
            dma((2,)),
            dma((2, CHUNKS)),
            dma,
            dma,
            dma((2,)),
            dma,
            dma,
            dma,
            dma,
            dma,
            dma,
        ],
        compiler_params=pltpu.CompilerParams(
            collective_id=0, has_side_effects=True, vmem_limit_bytes=52 * 2**20
        ),
        name="temporal_attention_backward",
    )(*flat, query_gain, key_gain)
    return (
        query_grad.reshape(shape),
        key_grad.reshape(shape),
        value_grad.reshape(shape),
        query_total,
        key_total,
    )


def solution(mesh):
    blocks = P("dp", "seq", None, None, None)
    gains = P("dp", None)
    return jax.shard_map(
        functools.partial(body, mesh.shape["dp"]),
        mesh=mesh,
        in_specs=(blocks, blocks, blocks, blocks, gains, gains),
        out_specs=(blocks, blocks, blocks, gains, gains),
        check_vma=False,
    )
```

```python
import functools
import math

import jax
import jax.numpy as jnp
from jax import lax
from jax.experimental import pallas as pl
from jax.experimental.pallas import tpu as pltpu
from jax.sharding import PartitionSpec as P

EPSILON = 1e-06
HEADS = 40
HDIM = 128
SEQ = 16
CHUNKS = 8
GROUP = 16
MESH = pl.DeviceIdType.MESH
NEGATIVE = -1e30


def peer_of(me, step):
    step = lax.rem(step * 9, SEQ)
    x = lax.rem(lax.div(me, 8) + lax.div(step, 8), 2)
    z = lax.rem(lax.div(me, 2) + lax.div(step, 2), 4)
    core = lax.rem(me + step, 2)
    return x * 8 + z * 2 + core


def kernel(
    dp_size,
    q_hbm, k_hbm, v_hbm, g_hbm, qgain_hbm, kgain_hbm,
    oq, ok, ov, total_gain,
    nrm, rcv, stg, ret, mask, gsend, gbuf, gain, acc, rsend, rbuf, asend, abuf,
    raw_sem, load_sem, fwd_send, fwd_recv, ret_send, ret_recv, val_send, val_recv,
    gain_send, gain_recv, rs_send, rs_recv, ag_send, ag_recv,
):
    me = lax.axis_index("seq")
    dp = lax.axis_index("dp")
    rows = q_hbm.shape[1]
    part = rows // CHUNKS
    local_heads = HEADS // dp_size
    pad = gsend.shape[0] // 2
    scaling = 1.0 / math.sqrt(HDIM)

    def remote(src, dst, send, recv, seq):
        return pltpu.make_async_remote_copy(
            src_ref=src, dst_ref=dst, send_sem=send, recv_sem=recv,
            device_id={"seq": seq}, device_id_type=MESH,
        )

    def remote_dp(src, dst, send, recv, other):
        return pltpu.make_async_remote_copy(
            src_ref=src, dst_ref=dst, send_sem=send, recv_sem=recv,
            device_id={"dp": other}, device_id_type=MESH,
        )

    held = (oq, ok)
    gsend[...] = jnp.zeros_like(gsend)
    gain_loads = [
        pltpu.make_async_copy(source, gsend.at[pl.ds(a * pad, local_heads)], load_sem.at[a])
        for a, source in enumerate((qgain_hbm, kgain_hbm))
    ]
    raw_loads = [
        pltpu.make_async_copy(source, held[a], raw_sem.at[a])
        for a, source in enumerate((q_hbm, k_hbm))
    ]
    for copy in gain_loads + raw_loads:
        copy.start()

    barrier = pltpu.get_barrier_semaphore()
    for step in range(1, SEQ):
        pl.semaphore_signal(
            barrier, inc=1, device_id={"seq": lax.rem(me + step, SEQ)}, device_id_type=MESH
        )
    for step in range(1, dp_size):
        pl.semaphore_signal(
            barrier, inc=1, device_id={"dp": lax.rem(dp + step, dp_size)}, device_id_type=MESH
        )
    pl.semaphore_wait(barrier, SEQ - 1 + dp_size - 1)

    for copy in gain_loads:
        copy.wait()
    for step in range(1, dp_size):
        remote_dp(
            gsend, gbuf.at[dp], gain_send, gain_recv, lax.rem(dp + step, dp_size)
        ).start()
    pltpu.make_async_copy(gsend, gbuf.at[dp], gain_recv).start()

    def send_values(c):
        here = pl.ds(c * part, part)

        def one(step, carry):
            seq = peer_of(me, step)
            for a, source in ((2, v_hbm), (3, g_hbm)):
                remote(
                    source.at[seq, here], rcv.at[a, c, me], fwd_send.at[a], fwd_recv.at[a, c], seq
                ).start()
            return carry

        lax.fori_loop(1, SEQ, one, 0)
        for a, source in ((2, v_hbm), (3, g_hbm)):
            pltpu.make_async_copy(source.at[me, here], rcv.at[a, c, me], fwd_recv.at[a, c]).start()

    def normalized(a, seq, here):
        wide = held[a][seq, here].astype(jnp.float32)
        inverse = lax.rsqrt(jnp.mean(wide * wide, axis=-1, keepdims=True) + EPSILON)
        return wide * inverse, inverse

    def by_head(tile, factor):
        split = tile.reshape(part // HEADS, HEADS, HDIM)
        return (split * factor[None]).reshape(part, HDIM)

    def send_normalized(c):
        here = pl.ds(c * part, part)

        def one(step, carry):
            seq = peer_of(me, step)
            for a in range(2):
                hat, _ = normalized(a, seq, here)
                nrm[a, seq, here] = by_head(hat, gain[a]).astype(jnp.bfloat16)

            @pl.when(step > 0)
            def _():
                for a in range(2):
                    remote(
                        nrm.at[a, seq, here], rcv.at[a, c, me],
                        fwd_send.at[a], fwd_recv.at[a, c], seq,
                    ).start()

            @pl.when(step == 0)
            def _():
                for a in range(2):
                    pltpu.make_async_copy(
                        nrm.at[a, me, here], rcv.at[a, c, me], fwd_recv.at[a, c]
                    ).start()

            return carry

        lax.fori_loop(0, SEQ, one, 0)

    send_values(0)
    row_ids = lax.broadcasted_iota(jnp.int32, mask.shape, 0)
    col_ids = lax.broadcasted_iota(jnp.int32, mask.shape, 1)
    allowed = (lax.rem(row_ids, GROUP) == lax.rem(col_ids, GROUP)) & (col_ids <= row_ids)
    mask[...] = jnp.where(allowed, 0.0, NEGATIVE)
    acc[...] = jnp.zeros_like(acc)

    pltpu.make_async_copy(gbuf, gbuf, gain_recv).wait()
    for d in range(dp_size):
        for a in range(2):
            gain[a, d * local_heads : (d + 1) * local_heads] = gbuf[
                d, a * pad : a * pad + local_heads
            ]
    for copy in raw_loads:
        copy.wait()

    send_normalized(0)
    for c in range(1, CHUNKS):
        send_values(c)
        send_normalized(c)

    def contract(left, right, dims):
        return lax.dot_general(left, right, (dims, ((), ())), preferred_element_type=jnp.float32)

    def attention(c):
        for a in range(4):
            pltpu.make_async_copy(rcv.at[a, c], rcv.at[a, c], fwd_recv.at[a, c]).wait()

        def block(b, carry):
            here = pl.ds(pl.multiple_of(b * GROUP, GROUP), GROUP)
            wide = SEQ * GROUP
            query, key, value, grad = (
                rcv[a, c, :, here, :].reshape(wide, HDIM) for a in range(4)
            )
            scores = contract(query, key, ((1,), (1,))) * scaling + mask[...]
            expo = jnp.exp(scores - jnp.max(scores, axis=-1, keepdims=True))
            probability = expo / jnp.sum(expo, axis=-1, keepdims=True)
            prob_low = probability.astype(jnp.bfloat16)
            prob_grad = contract(grad, value, ((1,), (1,)))
            row_dots = jnp.sum(prob_low.astype(jnp.float32) * prob_grad, axis=-1, keepdims=True)
            score_low = (probability * (prob_grad - row_dots)).astype(jnp.bfloat16)
            results = (
                contract(score_low, key, ((1,), (0,))) * scaling,
                contract(score_low, query, ((0,), (0,))) * scaling,
                contract(prob_low, grad, ((0,), (0,))),
            )
            for a, result in enumerate(results):
                stg[a, c, :, here, :] = result.astype(jnp.bfloat16).reshape(SEQ, GROUP, HDIM)
            return carry

        lax.fori_loop(0, part // GROUP, block, 0)

    def send_steps(c):
        def one(step, carry):
            seq = peer_of(me, step)
            for a in range(2):
                remote(
                    stg.at[a, c, seq], ret.at[a, c, me], ret_send.at[a], ret_recv.at[a, c], seq
                ).start()
            return carry

        lax.fori_loop(1, SEQ, one, 0)
        for a in range(2):
            pltpu.make_async_copy(stg.at[a, c, me], ret.at[a, c, me], ret_recv.at[a, c]).start()

    def send_value_grads(c):
        here = pl.ds(c * part, part)

        def one(step, carry):
            seq = peer_of(me, step)
            remote(stg.at[2, c, seq], ov.at[me, here], val_send, val_recv, seq).start()
            return carry

        lax.fori_loop(1, SEQ, one, 0)
        pltpu.make_async_copy(stg.at[2, c, me], ov.at[me, here], val_recv).start()

    def norm_back(c):
        here = pl.ds(c * part, part)
        for a in range(2):
            pltpu.make_async_copy(ret.at[a, c], ret.at[a, c], ret_recv.at[a, c]).wait()

        def one(seq, carry):
            for a in range(2):
                hat, inverse = normalized(a, seq, here)
                step = ret[a, c, seq].astype(jnp.float32)
                gained = by_head(step, gain[a])
                mean = jnp.mean(gained * hat, axis=-1, keepdims=True)
                held[a][seq, here] = (inverse * (gained - hat * mean)).astype(jnp.bfloat16)
                acc[a] += jnp.sum((step * hat).reshape(part // HEADS, HEADS, HDIM), axis=0)
            return carry

        lax.fori_loop(0, SEQ, one, 0)

    lots = (0, CHUNKS // 4, CHUNKS // 2, CHUNKS)

    def send_lot(lot):
        for c in range(lots[lot], lots[lot + 1]):
            send_value_grads(c)

    for c in range(CHUNKS):
        attention(c)
        send_steps(c)
    send_lot(0)
    for c in range(CHUNKS):
        norm_back(c)

    rsend[...] = jnp.zeros_like(rsend)
    for d in range(dp_size):
        for a in range(2):
            rsend[d, a * pad : a * pad + local_heads] = acc[
                a, d * local_heads : (d + 1) * local_heads
            ]
    for step in range(1, dp_size):
        other = lax.rem(dp + step, dp_size)
        remote_dp(rsend.at[other], rbuf.at[dp], rs_send, rs_recv, other).start()
    pltpu.make_async_copy(rsend.at[dp], rbuf.at[dp], rs_recv).start()
    send_lot(1)
    pltpu.make_async_copy(rbuf, rbuf, rs_recv).wait()
    asend[...] = jnp.sum(rbuf[...], axis=0)
    for step in range(1, SEQ):
        seq = lax.rem(me + step, SEQ)
        remote(asend, abuf.at[me], ag_send, ag_recv, seq).start()
    pltpu.make_async_copy(asend, abuf.at[me], ag_recv).start()
    send_lot(2)
    pltpu.make_async_copy(abuf, abuf, ag_recv).wait()
    total_gain[...] = jnp.sum(abuf[...], axis=0)

    others = pl.ds(0, SEQ - 1)
    pltpu.make_async_copy(ov, ov, val_recv).wait()
    for a in range(4):
        pltpu.make_async_copy(oq.at[others], oq.at[others], fwd_send.at[a]).wait()
    for a in range(2):
        pltpu.make_async_copy(oq.at[others], oq.at[others], ret_send.at[a]).wait()
    pltpu.make_async_copy(oq.at[others], oq.at[others], val_send).wait()
    if dp_size > 1:
        most = pl.ds(0, dp_size - 1)
        pltpu.make_async_copy(gbuf.at[most], gbuf.at[most], gain_send).wait()
        pltpu.make_async_copy(rbuf.at[most], rbuf.at[most], rs_send).wait()
    pltpu.make_async_copy(abuf.at[others], abuf.at[others], ag_send).wait()


def write_out(local_heads, oq, ok, ov, total_gain, *refs):
    outs, sems = refs[:5], refs[5]
    pad = total_gain.shape[0] // 2
    sources = (
        oq, ok, ov, total_gain.at[pl.ds(0, local_heads)], total_gain.at[pl.ds(pad, local_heads)]
    )
    copies = [
        pltpu.make_async_copy(source, out, sems.at[i])
        for i, (source, out) in enumerate(zip(sources, outs))
    ]
    for copy in copies:
        copy.start()
    for copy in copies:
        copy.wait()


def body(dp_size, queries, key_proj, value_proj, out_grad, query_gain, key_gain):
    shape = queries.shape
    rows = shape[2] * HEADS // SEQ
    part = rows // CHUNKS
    local_heads = query_gain.shape[0]
    pad = -(-local_heads // 8) * 8
    flat = [v.reshape(SEQ, rows, HDIM) for v in (queries, key_proj, value_proj, out_grad)]
    low, wide = jnp.bfloat16, jnp.float32
    anywhere = pl.BlockSpec(memory_space=pl.ANY)
    vmem = pl.BlockSpec(memory_space=pltpu.VMEM)
    dma = pltpu.SemaphoreType.DMA
    big = jax.ShapeDtypeStruct((SEQ, rows, HDIM), low)
    small = jax.ShapeDtypeStruct((local_heads, HDIM), wide)
    results = pl.pallas_call(
        functools.partial(kernel, dp_size),
        out_shape=(big, big, big, jax.ShapeDtypeStruct((2 * pad, HDIM), wide)),
        in_specs=[anywhere] * 6,
        out_specs=(vmem,) * 4,
        scratch_shapes=[
            pltpu.VMEM((2, SEQ, rows, HDIM), low),
            pltpu.VMEM((4, CHUNKS, SEQ, part, HDIM), low),
            pltpu.VMEM((3, CHUNKS, SEQ, part, HDIM), low),
            pltpu.VMEM((2, CHUNKS, SEQ, part, HDIM), low),
            pltpu.VMEM((SEQ * GROUP, SEQ * GROUP), wide),
            pltpu.VMEM((2 * pad, HDIM), wide),
            pltpu.VMEM((dp_size, 2 * pad, HDIM), wide),
            pltpu.VMEM((2, HEADS, HDIM), wide),
            pltpu.VMEM((2, HEADS, HDIM), wide),
            pltpu.VMEM((dp_size, 2 * pad, HDIM), wide),
            pltpu.VMEM((dp_size, 2 * pad, HDIM), wide),
            pltpu.VMEM((2 * pad, HDIM), wide),
            pltpu.VMEM((SEQ, 2 * pad, HDIM), wide),
            dma((2,)),
            dma((2,)),
            dma((4,)),
            dma((4, CHUNKS)),
            dma((2,)),
            dma((2, CHUNKS)),
            dma,
            dma,
            dma,
            dma,
            dma,
            dma,
            dma,
            dma,
        ],
        compiler_params=pltpu.CompilerParams(
            collective_id=0, has_side_effects=True, vmem_limit_bytes=44 * 2**20
        ),
        name="temporal_attention_backward",
    )(*flat, query_gain, key_gain)
    query_grad, key_grad, value_grad, query_total, key_total = pl.pallas_call(
        functools.partial(write_out, local_heads),
        out_shape=(big, big, big, small, small),
        in_specs=[vmem] * 4,
        out_specs=(anywhere,) * 5,
        scratch_shapes=[dma((5,))],
        compiler_params=pltpu.CompilerParams(vmem_limit_bytes=2**20),
        name="write_out",
    )(*results)
    return (
        query_grad.reshape(shape),
        key_grad.reshape(shape),
        value_grad.reshape(shape),
        query_total,
        key_total,
    )


def solution(mesh):
    blocks = P("dp", "seq", None, None, None)
    gains = P("dp", None)
    return jax.shard_map(
        functools.partial(body, mesh.shape["dp"]),
        mesh=mesh,
        in_specs=(blocks, blocks, blocks, blocks, gains, gains),
        out_specs=(blocks, blocks, blocks, gains, gains),
        check_vma=False,
    )
```

```python
import functools
import math

import jax
import jax.numpy as jnp
from jax import lax
from jax.experimental import pallas as pl
from jax.experimental.pallas import tpu as pltpu
from jax.sharding import PartitionSpec as P

EPSILON = 1e-06
HEADS = 40
HDIM = 128
SEQ = 16
CHUNKS = 8
GROUP = 16
MESH = pl.DeviceIdType.MESH
NEGATIVE = -1e30


def peer_of(me, step):
    step = lax.rem(step * 9, SEQ)
    x = lax.rem(lax.div(me, 8) + lax.div(step, 8), 2)
    z = lax.rem(lax.div(me, 2) + lax.div(step, 2), 4)
    core = lax.rem(me + step, 2)
    return x * 8 + z * 2 + core


def kernel(
    dp_size,
    q_hbm, k_hbm, v_hbm, g_hbm, qgain_hbm, kgain_hbm,
    oq, ok, ov, total_gain,
    nrm, rcv, stg, ret, mask, gsend, gbuf, gain, acc, rsend, rbuf, asend, abuf, row, bbuf,
    raw_sem, load_sem, fwd_send, fwd_recv, ret_send, ret_recv, val_send, val_recv,
    gain_send, gain_recv, rs_send, rs_recv, row_send, row_recv, ag_send, ag_recv,
):
    me = lax.axis_index("seq")
    dp = lax.axis_index("dp")
    rows = q_hbm.shape[1]
    part = rows // CHUNKS
    local_heads = HEADS // dp_size
    pad = SEQ // 2
    scaling = 1.0 / math.sqrt(HDIM)

    def remote(src, dst, send, recv, seq):
        return pltpu.make_async_remote_copy(
            src_ref=src, dst_ref=dst, send_sem=send, recv_sem=recv,
            device_id={"seq": seq}, device_id_type=MESH,
        )

    def remote_dp(src, dst, send, recv, other):
        return pltpu.make_async_remote_copy(
            src_ref=src, dst_ref=dst, send_sem=send, recv_sem=recv,
            device_id={"dp": other}, device_id_type=MESH,
        )

    held = (oq, ok)
    gsend[...] = jnp.zeros_like(gsend)
    gain_loads = [
        pltpu.make_async_copy(source, gsend.at[pl.ds(a * pad, local_heads)], load_sem.at[a])
        for a, source in enumerate((qgain_hbm, kgain_hbm))
    ]
    raw_loads = [
        pltpu.make_async_copy(source, held[a], raw_sem.at[a])
        for a, source in enumerate((q_hbm, k_hbm))
    ]
    for copy in gain_loads + raw_loads:
        copy.start()

    barrier = pltpu.get_barrier_semaphore()
    for step in range(1, SEQ):
        pl.semaphore_signal(
            barrier, inc=1, device_id={"seq": lax.rem(me + step, SEQ)}, device_id_type=MESH
        )
    for step in range(1, dp_size):
        pl.semaphore_signal(
            barrier, inc=1, device_id={"dp": lax.rem(dp + step, dp_size)}, device_id_type=MESH
        )
    pl.semaphore_wait(barrier, SEQ - 1 + dp_size - 1)

    for copy in gain_loads:
        copy.wait()
    for step in range(1, dp_size):
        remote_dp(
            gsend, gbuf.at[dp], gain_send, gain_recv, lax.rem(dp + step, dp_size)
        ).start()
    pltpu.make_async_copy(gsend, gbuf.at[dp], gain_recv).start()

    def send_values(c):
        here = pl.ds(c * part, part)

        def one(step, carry):
            seq = peer_of(me, step)
            for a, source in ((2, v_hbm), (3, g_hbm)):
                remote(
                    source.at[seq, here], rcv.at[a, c, me], fwd_send.at[a], fwd_recv.at[a, c], seq
                ).start()
            return carry

        lax.fori_loop(1, SEQ, one, 0)
        for a, source in ((2, v_hbm), (3, g_hbm)):
            pltpu.make_async_copy(source.at[me, here], rcv.at[a, c, me], fwd_recv.at[a, c]).start()

    def normalized(a, seq, here):
        wide = held[a][seq, here].astype(jnp.float32)
        inverse = lax.rsqrt(jnp.mean(wide * wide, axis=-1, keepdims=True) + EPSILON)
        return wide * inverse, inverse

    def by_head(tile, factor):
        split = tile.reshape(part // HEADS, HEADS, HDIM)
        return (split * factor[None]).reshape(part, HDIM)

    def send_normalized(c):
        here = pl.ds(c * part, part)

        def one(step, carry):
            seq = peer_of(me, step)
            for a in range(2):
                hat, _ = normalized(a, seq, here)
                nrm[a, seq, here] = by_head(hat, gain[a]).astype(jnp.bfloat16)

            @pl.when(step > 0)
            def _():
                for a in range(2):
                    remote(
                        nrm.at[a, seq, here], rcv.at[a, c, me],
                        fwd_send.at[a], fwd_recv.at[a, c], seq,
                    ).start()

            @pl.when(step == 0)
            def _():
                for a in range(2):
                    pltpu.make_async_copy(
                        nrm.at[a, me, here], rcv.at[a, c, me], fwd_recv.at[a, c]
                    ).start()

            return carry

        lax.fori_loop(0, SEQ, one, 0)

    send_values(0)
    row_ids = lax.broadcasted_iota(jnp.int32, mask.shape, 0)
    col_ids = lax.broadcasted_iota(jnp.int32, mask.shape, 1)
    allowed = (lax.rem(row_ids, GROUP) == lax.rem(col_ids, GROUP)) & (col_ids <= row_ids)
    mask[...] = jnp.where(allowed, 0.0, NEGATIVE)
    acc[...] = jnp.zeros_like(acc)

    pltpu.make_async_copy(gbuf, gbuf, gain_recv).wait()
    for d in range(dp_size):
        for a in range(2):
            gain[a, d * local_heads : (d + 1) * local_heads] = gbuf[
                d, a * pad : a * pad + local_heads
            ]
    for copy in raw_loads:
        copy.wait()

    send_normalized(0)
    for c in range(1, CHUNKS):
        send_values(c)
        send_normalized(c)

    def contract(left, right, dims):
        return lax.dot_general(left, right, (dims, ((), ())), preferred_element_type=jnp.float32)

    def attention(c):
        for a in range(4):
            pltpu.make_async_copy(rcv.at[a, c], rcv.at[a, c], fwd_recv.at[a, c]).wait()

        def block(b, carry):
            here = pl.ds(pl.multiple_of(b * GROUP, GROUP), GROUP)
            wide = SEQ * GROUP
            query, key, value, grad = (
                rcv[a, c, :, here, :].reshape(wide, HDIM) for a in range(4)
            )
            scores = contract(query, key, ((1,), (1,))) * scaling + mask[...]
            expo = jnp.exp(scores - jnp.max(scores, axis=-1, keepdims=True))
            probability = expo / jnp.sum(expo, axis=-1, keepdims=True)
            prob_low = probability.astype(jnp.bfloat16)
            prob_grad = contract(grad, value, ((1,), (1,)))
            row_dots = jnp.sum(prob_low.astype(jnp.float32) * prob_grad, axis=-1, keepdims=True)
            score_low = (probability * (prob_grad - row_dots)).astype(jnp.bfloat16)
            results = (
                contract(score_low, key, ((1,), (0,))) * scaling,
                contract(score_low, query, ((0,), (0,))) * scaling,
                contract(prob_low, grad, ((0,), (0,))),
            )
            for a, result in enumerate(results):
                stg[a, c, :, here, :] = result.astype(jnp.bfloat16).reshape(SEQ, GROUP, HDIM)
            return carry

        lax.fori_loop(0, part // GROUP, block, 0)

    def send_steps(c):
        def one(step, carry):
            seq = peer_of(me, step)
            for a in range(2):
                remote(
                    stg.at[a, c, seq], ret.at[a, c, me], ret_send.at[a], ret_recv.at[a, c], seq
                ).start()
            return carry

        lax.fori_loop(1, SEQ, one, 0)
        for a in range(2):
            pltpu.make_async_copy(stg.at[a, c, me], ret.at[a, c, me], ret_recv.at[a, c]).start()

    def send_value_grads(c):
        here = pl.ds(c * part, part)

        def one(step, carry):
            seq = peer_of(me, step)
            remote(stg.at[2, c, seq], ov.at[me, here], val_send, val_recv, seq).start()
            return carry

        lax.fori_loop(1, SEQ, one, 0)
        pltpu.make_async_copy(stg.at[2, c, me], ov.at[me, here], val_recv).start()

    def norm_back(c):
        here = pl.ds(c * part, part)
        for a in range(2):
            pltpu.make_async_copy(ret.at[a, c], ret.at[a, c], ret_recv.at[a, c]).wait()

        def one(seq, carry):
            for a in range(2):
                hat, inverse = normalized(a, seq, here)
                step = ret[a, c, seq].astype(jnp.float32)
                gained = by_head(step, gain[a])
                mean = jnp.mean(gained * hat, axis=-1, keepdims=True)
                held[a][seq, here] = (inverse * (gained - hat * mean)).astype(jnp.bfloat16)
                acc[a] += jnp.sum((step * hat).reshape(part // HEADS, HEADS, HDIM), axis=0)
            return carry

        lax.fori_loop(0, SEQ, one, 0)

    lots = (0, CHUNKS // 4, CHUNKS // 2, 3 * CHUNKS // 4, CHUNKS)

    def send_lot(lot):
        for c in range(lots[lot], lots[lot + 1]):
            send_value_grads(c)

    for c in range(CHUNKS):
        attention(c)
        send_steps(c)
    send_lot(0)
    for c in range(CHUNKS):
        norm_back(c)

    rsend[...] = jnp.zeros_like(rsend)
    for d in range(dp_size):
        for a in range(2):
            rsend[d, a * pad : a * pad + local_heads] = acc[
                a, d * local_heads : (d + 1) * local_heads
            ]
    for step in range(1, dp_size):
        other = lax.rem(dp + step, dp_size)
        remote_dp(rsend.at[other], rbuf.at[dp], rs_send, rs_recv, other).start()
    pltpu.make_async_copy(rsend.at[dp], rbuf.at[dp], rs_recv).start()
    send_lot(1)
    pltpu.make_async_copy(rbuf, rbuf, rs_recv).wait()
    asend[...] = jnp.sum(rbuf[...], axis=0).reshape(asend.shape)
    for step in range(1, SEQ):
        seq = lax.rem(me + step, SEQ)
        remote(asend.at[seq], abuf.at[me], row_send, row_recv, seq).start()
    pltpu.make_async_copy(asend.at[me], abuf.at[me], row_recv).start()
    send_lot(2)
    pltpu.make_async_copy(abuf, abuf, row_recv).wait()
    row[...] = jnp.sum(abuf[...], axis=0)
    for step in range(1, SEQ):
        seq = lax.rem(me + step, SEQ)
        remote(row, bbuf.at[me], ag_send, ag_recv, seq).start()
    pltpu.make_async_copy(row, bbuf.at[me], ag_recv).start()
    send_lot(3)
    pltpu.make_async_copy(bbuf, bbuf, ag_recv).wait()
    total_gain[...] = bbuf[...].reshape(total_gain.shape)

    others = pl.ds(0, SEQ - 1)
    pltpu.make_async_copy(ov, ov, val_recv).wait()
    for a in range(4):
        pltpu.make_async_copy(oq.at[others], oq.at[others], fwd_send.at[a]).wait()
    for a in range(2):
        pltpu.make_async_copy(oq.at[others], oq.at[others], ret_send.at[a]).wait()
    pltpu.make_async_copy(oq.at[others], oq.at[others], val_send).wait()
    if dp_size > 1:
        most = pl.ds(0, dp_size - 1)
        pltpu.make_async_copy(gbuf.at[most], gbuf.at[most], gain_send).wait()
        pltpu.make_async_copy(rbuf.at[most], rbuf.at[most], rs_send).wait()
    pltpu.make_async_copy(abuf.at[others], abuf.at[others], row_send).wait()
    pltpu.make_async_copy(bbuf.at[others], bbuf.at[others], ag_send).wait()


def write_out(local_heads, oq, ok, ov, total_gain, *refs):
    outs, sems = refs[:5], refs[5]
    pad = total_gain.shape[0] // 2
    quarter = SEQ // 4
    copies = [
        pltpu.make_async_copy(source.at[here], out.at[here], sems.at[i, n])
        for n, here in enumerate(pl.ds(q * quarter, quarter) for q in range(4))
        for i, (source, out) in enumerate(zip((oq, ok, ov), outs))
    ]
    for a in range(2):
        source = total_gain.at[pl.ds(a * pad, local_heads)]
        copies.append(pltpu.make_async_copy(source, outs[3 + a], sems.at[3, a]))
    for copy in copies:
        copy.start()
    for copy in copies:
        copy.wait()


def body(dp_size, queries, key_proj, value_proj, out_grad, query_gain, key_gain):
    shape = queries.shape
    rows = shape[2] * HEADS // SEQ
    part = rows // CHUNKS
    local_heads = query_gain.shape[0]
    pad = SEQ // 2
    flat = [v.reshape(SEQ, rows, HDIM) for v in (queries, key_proj, value_proj, out_grad)]
    low, wide = jnp.bfloat16, jnp.float32
    anywhere = pl.BlockSpec(memory_space=pl.ANY)
    vmem = pl.BlockSpec(memory_space=pltpu.VMEM)
    dma = pltpu.SemaphoreType.DMA
    big = jax.ShapeDtypeStruct((SEQ, rows, HDIM), low)
    small = jax.ShapeDtypeStruct((local_heads, HDIM), wide)
    results = pl.pallas_call(
        functools.partial(kernel, dp_size),
        out_shape=(big, big, big, jax.ShapeDtypeStruct((2 * pad, HDIM), wide)),
        in_specs=[anywhere] * 6,
        out_specs=(vmem,) * 4,
        scratch_shapes=[
            pltpu.VMEM((2, SEQ, rows, HDIM), low),
            pltpu.VMEM((4, CHUNKS, SEQ, part, HDIM), low),
            pltpu.VMEM((3, CHUNKS, SEQ, part, HDIM), low),
            pltpu.VMEM((2, CHUNKS, SEQ, part, HDIM), low),
            pltpu.VMEM((SEQ * GROUP, SEQ * GROUP), wide),
            pltpu.VMEM((2 * pad, HDIM), wide),
            pltpu.VMEM((dp_size, 2 * pad, HDIM), wide),
            pltpu.VMEM((2, HEADS, HDIM), wide),
            pltpu.VMEM((2, HEADS, HDIM), wide),
            pltpu.VMEM((dp_size, 2 * pad, HDIM), wide),
            pltpu.VMEM((dp_size, 2 * pad, HDIM), wide),
            pltpu.VMEM((SEQ, 1, HDIM), wide),
            pltpu.VMEM((SEQ, 1, HDIM), wide),
            pltpu.VMEM((1, HDIM), wide),
            pltpu.VMEM((SEQ, 1, HDIM), wide),
            dma((2,)),
            dma((2,)),
            dma((4,)),
            dma((4, CHUNKS)),
            dma((2,)),
            dma((2, CHUNKS)),
            dma,
            dma,
            dma,
            dma,
            dma,
            dma,
            dma,
            dma,
            dma,
            dma,
        ],
        compiler_params=pltpu.CompilerParams(
            collective_id=0, has_side_effects=True, vmem_limit_bytes=44 * 2**20
        ),
        name="temporal_attention_backward",
    )(*flat, query_gain, key_gain)
    query_grad, key_grad, value_grad, query_total, key_total = pl.pallas_call(
        functools.partial(write_out, local_heads),
        out_shape=(big, big, big, small, small),
        in_specs=[vmem] * 4,
        out_specs=(anywhere,) * 5,
        scratch_shapes=[dma((4, 4))],
        compiler_params=pltpu.CompilerParams(vmem_limit_bytes=2**20),
        name="write_out",
    )(*results)
    return (
        query_grad.reshape(shape),
        key_grad.reshape(shape),
        value_grad.reshape(shape),
        query_total,
        key_total,
    )


def solution(mesh):
    blocks = P("dp", "seq", None, None, None)
    gains = P("dp", None)
    return jax.shard_map(
        functools.partial(body, mesh.shape["dp"]),
        mesh=mesh,
        in_specs=(blocks, blocks, blocks, blocks, gains, gains),
        out_specs=(blocks, blocks, blocks, gains, gains),
        check_vma=False,
    )
```

```python
import functools
import math

import jax
import jax.numpy as jnp
from jax import lax
from jax.experimental import pallas as pl
from jax.experimental.pallas import tpu as pltpu
from jax.sharding import PartitionSpec as P

EPSILON = 1e-06
HEADS = 40
HDIM = 128
SEQ = 16
CHUNKS = 8
GROUP = 16
MESH = pl.DeviceIdType.MESH
NEGATIVE = -1e30


def peer_of(me, step):
    step = lax.rem(step * 9, SEQ)
    x = lax.rem(lax.div(me, 8) + lax.div(step, 8), 2)
    z = lax.rem(lax.div(me, 2) + lax.div(step, 2), 4)
    core = lax.rem(me + step, 2)
    return x * 8 + z * 2 + core


def kernel(
    dp_size,
    q_hbm, k_hbm, v_hbm, g_hbm, gains_hbm,
    oq, ok, ov, total_gain,
    nrm, rcv, stg, ret, mask, gsend, gbuf, gain, acc, rsend, rbuf, asend, abuf, row, bbuf,
    raw_sem, load_sem, fwd_send, fwd_recv, ret_send, ret_recv, val_send, val_recv,
    gain_send, gain_recv, rs_send, rs_recv, row_send, row_recv, ag_send, ag_recv,
):
    me = lax.axis_index("seq")
    dp = lax.axis_index("dp")
    rows = q_hbm.shape[1]
    part = rows // CHUNKS
    local_heads = HEADS // dp_size
    pad = SEQ // 2
    scaling = 1.0 / math.sqrt(HDIM)

    def remote(src, dst, send, recv, seq):
        return pltpu.make_async_remote_copy(
            src_ref=src, dst_ref=dst, send_sem=send, recv_sem=recv,
            device_id={"seq": seq}, device_id_type=MESH,
        )

    def remote_dp(src, dst, send, recv, other):
        return pltpu.make_async_remote_copy(
            src_ref=src, dst_ref=dst, send_sem=send, recv_sem=recv,
            device_id={"dp": other}, device_id_type=MESH,
        )

    barrier = pltpu.get_barrier_semaphore()
    for step in range(1, SEQ):
        pl.semaphore_signal(
            barrier, inc=1, device_id={"seq": lax.rem(me + step, SEQ)}, device_id_type=MESH
        )
    for step in range(1, dp_size):
        pl.semaphore_signal(
            barrier, inc=1, device_id={"dp": lax.rem(dp + step, dp_size)}, device_id_type=MESH
        )

    held = (oq, ok)
    gain_loads = [pltpu.make_async_copy(gains_hbm, gsend, load_sem)]
    raw_loads = [
        pltpu.make_async_copy(source, held[a], raw_sem.at[a])
        for a, source in enumerate((q_hbm, k_hbm))
    ]
    for copy in gain_loads + raw_loads:
        copy.start()

    pl.semaphore_wait(barrier, SEQ - 1 + dp_size - 1)

    for copy in gain_loads:
        copy.wait()
    for step in range(1, dp_size):
        remote_dp(
            gsend, gbuf.at[dp], gain_send, gain_recv, lax.rem(dp + step, dp_size)
        ).start()
    pltpu.make_async_copy(gsend, gbuf.at[dp], gain_recv).start()

    def send_values(c):
        here = pl.ds(c * part, part)

        def one(step, carry):
            seq = peer_of(me, step)
            for a, source in ((2, v_hbm), (3, g_hbm)):
                remote(
                    source.at[seq, here], rcv.at[a, c, me], fwd_send.at[a], fwd_recv.at[a, c], seq
                ).start()
            return carry

        lax.fori_loop(1, SEQ, one, 0)
        for a, source in ((2, v_hbm), (3, g_hbm)):
            pltpu.make_async_copy(source.at[me, here], rcv.at[a, c, me], fwd_recv.at[a, c]).start()

    def normalized(a, seq, here):
        wide = held[a][seq, here].astype(jnp.float32)
        inverse = lax.rsqrt(jnp.mean(wide * wide, axis=-1, keepdims=True) + EPSILON)
        return wide * inverse, inverse

    def by_head(tile, factor):
        split = tile.reshape(part // HEADS, HEADS, HDIM)
        return (split * factor[None]).reshape(part, HDIM)

    def send_normalized(c):
        here = pl.ds(c * part, part)

        def one(step, carry):
            seq = peer_of(me, step)
            for a in range(2):
                hat, _ = normalized(a, seq, here)
                nrm[a, seq, here] = by_head(hat, gain[a]).astype(jnp.bfloat16)

            @pl.when(step > 0)
            def _():
                for a in range(2):
                    remote(
                        nrm.at[a, seq, here], rcv.at[a, c, me],
                        fwd_send.at[a], fwd_recv.at[a, c], seq,
                    ).start()

            @pl.when(step == 0)
            def _():
                for a in range(2):
                    pltpu.make_async_copy(
                        nrm.at[a, me, here], rcv.at[a, c, me], fwd_recv.at[a, c]
                    ).start()

            return carry

        lax.fori_loop(0, SEQ, one, 0)

    send_values(0)
    row_ids = lax.broadcasted_iota(jnp.int32, mask.shape, 0)
    col_ids = lax.broadcasted_iota(jnp.int32, mask.shape, 1)
    allowed = (lax.rem(row_ids, GROUP) == lax.rem(col_ids, GROUP)) & (col_ids <= row_ids)
    mask[...] = jnp.where(allowed, 0.0, NEGATIVE)
    acc[...] = jnp.zeros_like(acc)

    pltpu.make_async_copy(gbuf, gbuf, gain_recv).wait()
    for d in range(dp_size):
        for a in range(2):
            gain[a, d * local_heads : (d + 1) * local_heads] = gbuf[
                d, a * pad : a * pad + local_heads
            ]
    for copy in raw_loads:
        copy.wait()

    send_normalized(0)
    for c in range(1, CHUNKS):
        send_values(c)
        send_normalized(c)

    def contract(left, right, dims):
        return lax.dot_general(left, right, (dims, ((), ())), preferred_element_type=jnp.float32)

    def attention(c):
        for a in range(4):
            pltpu.make_async_copy(rcv.at[a, c], rcv.at[a, c], fwd_recv.at[a, c]).wait()

        def block(b, carry):
            here = pl.ds(pl.multiple_of(b * GROUP, GROUP), GROUP)
            wide = SEQ * GROUP
            query, key, value, grad = (
                rcv[a, c, :, here, :].reshape(wide, HDIM) for a in range(4)
            )
            scores = contract(query, key, ((1,), (1,))) * scaling + mask[...]
            expo = jnp.exp(scores - jnp.max(scores, axis=-1, keepdims=True))
            probability = expo / jnp.sum(expo, axis=-1, keepdims=True)
            prob_low = probability.astype(jnp.bfloat16)
            prob_grad = contract(grad, value, ((1,), (1,)))
            row_dots = jnp.sum(prob_low.astype(jnp.float32) * prob_grad, axis=-1, keepdims=True)
            score_low = (probability * (prob_grad - row_dots)).astype(jnp.bfloat16)
            results = (
                contract(score_low, key, ((1,), (0,))) * scaling,
                contract(score_low, query, ((0,), (0,))) * scaling,
                contract(prob_low, grad, ((0,), (0,))),
            )
            for a, result in enumerate(results):
                stg[a, c, :, here, :] = result.astype(jnp.bfloat16).reshape(SEQ, GROUP, HDIM)
            return carry

        lax.fori_loop(0, part // GROUP, block, 0)

    def send_steps(c):
        def one(step, carry):
            seq = peer_of(me, step)
            for a in range(2):
                remote(
                    stg.at[a, c, seq], ret.at[a, c, me], ret_send.at[a], ret_recv.at[a, c], seq
                ).start()
            return carry

        lax.fori_loop(1, SEQ, one, 0)
        for a in range(2):
            pltpu.make_async_copy(stg.at[a, c, me], ret.at[a, c, me], ret_recv.at[a, c]).start()

    def send_value_grads(c):
        here = pl.ds(c * part, part)

        def one(step, carry):
            seq = peer_of(me, step)
            remote(stg.at[2, c, seq], ov.at[me, here], val_send, val_recv, seq).start()
            return carry

        lax.fori_loop(1, SEQ, one, 0)
        pltpu.make_async_copy(stg.at[2, c, me], ov.at[me, here], val_recv).start()

    def norm_back(c):
        here = pl.ds(c * part, part)
        for a in range(2):
            pltpu.make_async_copy(ret.at[a, c], ret.at[a, c], ret_recv.at[a, c]).wait()

        def one(seq, carry):
            for a in range(2):
                hat, inverse = normalized(a, seq, here)
                step = ret[a, c, seq].astype(jnp.float32)
                gained = by_head(step, gain[a])
                mean = jnp.mean(gained * hat, axis=-1, keepdims=True)
                held[a][seq, here] = (inverse * (gained - hat * mean)).astype(jnp.bfloat16)
                acc[a] += jnp.sum((step * hat).reshape(part // HEADS, HEADS, HDIM), axis=0)
            return carry

        lax.fori_loop(0, SEQ, one, 0)

    lots = (0, CHUNKS // 4, CHUNKS // 2, 3 * CHUNKS // 4, CHUNKS)

    def send_lot(lot):
        for c in range(lots[lot], lots[lot + 1]):
            send_value_grads(c)

    for c in range(CHUNKS):
        attention(c)
        send_steps(c)
    send_lot(0)
    for c in range(CHUNKS):
        norm_back(c)

    rsend[...] = jnp.zeros_like(rsend)
    for d in range(dp_size):
        for a in range(2):
            rsend[d, a * pad : a * pad + local_heads] = acc[
                a, d * local_heads : (d + 1) * local_heads
            ]
    for step in range(1, dp_size):
        other = lax.rem(dp + step, dp_size)
        remote_dp(rsend.at[other], rbuf.at[dp], rs_send, rs_recv, other).start()
    pltpu.make_async_copy(rsend.at[dp], rbuf.at[dp], rs_recv).start()
    send_lot(1)
    pltpu.make_async_copy(rbuf, rbuf, rs_recv).wait()
    asend[...] = jnp.sum(rbuf[...], axis=0).reshape(asend.shape)
    for step in range(1, SEQ):
        seq = lax.rem(me + step, SEQ)
        remote(asend.at[seq], abuf.at[me], row_send, row_recv, seq).start()
    pltpu.make_async_copy(asend.at[me], abuf.at[me], row_recv).start()
    send_lot(2)
    pltpu.make_async_copy(abuf, abuf, row_recv).wait()
    row[...] = jnp.sum(abuf[...], axis=0)
    for step in range(1, SEQ):
        seq = lax.rem(me + step, SEQ)
        remote(row, bbuf.at[me], ag_send, ag_recv, seq).start()
    pltpu.make_async_copy(row, bbuf.at[me], ag_recv).start()
    send_lot(3)
    pltpu.make_async_copy(bbuf, bbuf, ag_recv).wait()
    total_gain[...] = bbuf[...].reshape(total_gain.shape)

    others = pl.ds(0, SEQ - 1)
    pltpu.make_async_copy(ov, ov, val_recv).wait()
    for a in range(4):
        pltpu.make_async_copy(oq.at[others], oq.at[others], fwd_send.at[a]).wait()
    for a in range(2):
        pltpu.make_async_copy(oq.at[others], oq.at[others], ret_send.at[a]).wait()
    pltpu.make_async_copy(oq.at[others], oq.at[others], val_send).wait()
    if dp_size > 1:
        most = pl.ds(0, dp_size - 1)
        pltpu.make_async_copy(gbuf.at[most], gbuf.at[most], gain_send).wait()
        pltpu.make_async_copy(rbuf.at[most], rbuf.at[most], rs_send).wait()
    pltpu.make_async_copy(abuf.at[others], abuf.at[others], row_send).wait()
    pltpu.make_async_copy(bbuf.at[others], bbuf.at[others], ag_send).wait()


def write_out(local_heads, oq, ok, ov, total_gain, *refs):
    outs, sems = refs[:5], refs[5]
    pad = total_gain.shape[0] // 2
    quarter = SEQ // 4
    copies = [
        pltpu.make_async_copy(source.at[here], out.at[here], sems.at[i, n])
        for n, here in enumerate(pl.ds(q * quarter, quarter) for q in range(4))
        for i, (source, out) in enumerate(zip((oq, ok, ov), outs))
    ]
    for a in range(2):
        source = total_gain.at[pl.ds(a * pad, local_heads)]
        copies.append(pltpu.make_async_copy(source, outs[3 + a], sems.at[3, a]))
    for copy in copies:
        copy.start()
    for copy in copies:
        copy.wait()


def body(dp_size, queries, key_proj, value_proj, out_grad, query_gain, key_gain):
    shape = queries.shape
    rows = shape[2] * HEADS // SEQ
    part = rows // CHUNKS
    local_heads = query_gain.shape[0]
    pad = SEQ // 2
    flat = [v.reshape(SEQ, rows, HDIM) for v in (queries, key_proj, value_proj, out_grad)]
    low, wide = jnp.bfloat16, jnp.float32
    gap = ((0, pad - local_heads), (0, 0))
    gains = jnp.concatenate([jnp.pad(query_gain, gap), jnp.pad(key_gain, gap)], axis=0)
    anywhere = pl.BlockSpec(memory_space=pl.ANY)
    vmem = pl.BlockSpec(memory_space=pltpu.VMEM)
    dma = pltpu.SemaphoreType.DMA
    big = jax.ShapeDtypeStruct((SEQ, rows, HDIM), low)
    small = jax.ShapeDtypeStruct((local_heads, HDIM), wide)
    results = pl.pallas_call(
        functools.partial(kernel, dp_size),
        out_shape=(big, big, big, jax.ShapeDtypeStruct((2 * pad, HDIM), wide)),
        in_specs=[anywhere] * 5,
        out_specs=(vmem,) * 4,
        scratch_shapes=[
            pltpu.VMEM((2, SEQ, rows, HDIM), low),
            pltpu.VMEM((4, CHUNKS, SEQ, part, HDIM), low),
            pltpu.VMEM((3, CHUNKS, SEQ, part, HDIM), low),
            pltpu.VMEM((2, CHUNKS, SEQ, part, HDIM), low),
            pltpu.VMEM((SEQ * GROUP, SEQ * GROUP), wide),
            pltpu.VMEM((2 * pad, HDIM), wide),
            pltpu.VMEM((dp_size, 2 * pad, HDIM), wide),
            pltpu.VMEM((2, HEADS, HDIM), wide),
            pltpu.VMEM((2, HEADS, HDIM), wide),
            pltpu.VMEM((dp_size, 2 * pad, HDIM), wide),
            pltpu.VMEM((dp_size, 2 * pad, HDIM), wide),
            pltpu.VMEM((SEQ, 1, HDIM), wide),
            pltpu.VMEM((SEQ, 1, HDIM), wide),
            pltpu.VMEM((1, HDIM), wide),
            pltpu.VMEM((SEQ, 1, HDIM), wide),
            dma((2,)),
            dma,
            dma((4,)),
            dma((4, CHUNKS)),
            dma((2,)),
            dma((2, CHUNKS)),
            dma,
            dma,
            dma,
            dma,
            dma,
            dma,
            dma,
            dma,
            dma,
            dma,
        ],
        compiler_params=pltpu.CompilerParams(
            collective_id=0, has_side_effects=True, vmem_limit_bytes=44 * 2**20
        ),
        name="temporal_attention_backward",
    )(*flat, gains)
    query_grad, key_grad, value_grad, query_total, key_total = pl.pallas_call(
        functools.partial(write_out, local_heads),
        out_shape=(big, big, big, small, small),
        in_specs=[vmem] * 4,
        out_specs=(anywhere,) * 5,
        scratch_shapes=[dma((4, 4))],
        compiler_params=pltpu.CompilerParams(vmem_limit_bytes=2**20),
        name="write_out",
    )(*results)
    return (
        query_grad.reshape(shape),
        key_grad.reshape(shape),
        value_grad.reshape(shape),
        query_total,
        key_total,
    )


def solution(mesh):
    blocks = P("dp", "seq", None, None, None)
    gains = P("dp", None)
    return jax.shard_map(
        functools.partial(body, mesh.shape["dp"]),
        mesh=mesh,
        in_specs=(blocks, blocks, blocks, blocks, gains, gains),
        out_specs=(blocks, blocks, blocks, gains, gains),
        check_vma=False,
    )
```

```python
import functools
import math

import jax
import jax.numpy as jnp
from jax import lax
from jax.experimental import pallas as pl
from jax.experimental.pallas import tpu as pltpu
from jax.sharding import PartitionSpec as P

EPSILON = 1e-06
HEADS = 40
HDIM = 128
SEQ = 16
CHUNKS = 8
GROUP = 16
MESH = pl.DeviceIdType.MESH
NEGATIVE = -1e30


def peer_of(me, step):
    step = lax.rem(step * 9, SEQ)
    x = lax.rem(lax.div(me, 8) + lax.div(step, 8), 2)
    z = lax.rem(lax.div(me, 2) + lax.div(step, 2), 4)
    core = lax.rem(me + step, 2)
    return x * 8 + z * 2 + core


def kernel(
    dp_size,
    q_hbm, k_hbm, v_hbm, g_hbm, gains_hbm,
    oq, ok, ov, total_gain,
    nrm, rcv, stg, ret, mask, gsend, gbuf, gain, acc, rsend, rbuf, asend, abuf, row, bbuf,
    raw_sem, load_sem, fwd_send, fwd_recv, ret_send, ret_recv, val_send, val_recv,
    gain_send, gain_recv, rs_send, rs_recv, row_send, row_recv, ag_send, ag_recv,
    ready, everyone,
):
    me = lax.axis_index("seq")
    dp = lax.axis_index("dp")
    rows = q_hbm.shape[1]
    part = rows // CHUNKS
    local_heads = HEADS // dp_size
    pad = SEQ // 2
    scaling = 1.0 / math.sqrt(HDIM)

    def remote(src, dst, send, recv, seq):
        return pltpu.make_async_remote_copy(
            src_ref=src, dst_ref=dst, send_sem=send, recv_sem=recv,
            device_id={"seq": seq}, device_id_type=MESH,
        )

    def remote_dp(src, dst, send, recv, other):
        return pltpu.make_async_remote_copy(
            src_ref=src, dst_ref=dst, send_sem=send, recv_sem=recv,
            device_id={"dp": other}, device_id_type=MESH,
        )

    barrier = pltpu.get_barrier_semaphore()
    for step in range(1, SEQ):
        pl.semaphore_signal(
            barrier, inc=1, device_id={"seq": lax.rem(me + step, SEQ)}, device_id_type=MESH
        )

    @pl.when(me == 0)
    def _():
        for step in range(1, dp_size):
            pl.semaphore_signal(
                barrier, inc=1, device_id={"dp": lax.rem(dp + step, dp_size)}, device_id_type=MESH
            )

    held = (oq, ok)
    gain_loads = [pltpu.make_async_copy(gains_hbm, gsend, load_sem)]
    raw_loads = [
        pltpu.make_async_copy(source, held[a], raw_sem.at[a])
        for a, source in enumerate((q_hbm, k_hbm))
    ]
    for copy in gain_loads + raw_loads:
        copy.start()

    @pl.when(me == 0)
    def _():
        pl.semaphore_wait(barrier, SEQ - 1 + dp_size - 1)

    @pl.when(me > 0)
    def _():
        pl.semaphore_wait(barrier, SEQ - 1)

    def send_values(c):
        here = pl.ds(c * part, part)

        def one(step, carry):
            seq = peer_of(me, step)
            for a, source in ((2, v_hbm), (3, g_hbm)):
                remote(
                    source.at[seq, here], rcv.at[a, c, me], fwd_send.at[a], fwd_recv.at[a, c], seq
                ).start()
            return carry

        lax.fori_loop(1, SEQ, one, 0)
        for a, source in ((2, v_hbm), (3, g_hbm)):
            pltpu.make_async_copy(source.at[me, here], rcv.at[a, c, me], fwd_recv.at[a, c]).start()

    def normalized(a, seq, here):
        wide = held[a][seq, here].astype(jnp.float32)
        inverse = lax.rsqrt(jnp.mean(wide * wide, axis=-1, keepdims=True) + EPSILON)
        return wide * inverse, inverse

    def by_head(tile, factor):
        split = tile.reshape(part // HEADS, HEADS, HDIM)
        return (split * factor[None]).reshape(part, HDIM)

    def send_normalized(c):
        here = pl.ds(c * part, part)

        def one(step, carry):
            seq = peer_of(me, step)
            for a in range(2):
                hat, _ = normalized(a, seq, here)
                nrm[a, seq, here] = by_head(hat, gain[a]).astype(jnp.bfloat16)

            @pl.when(step > 0)
            def _():
                for a in range(2):
                    remote(
                        nrm.at[a, seq, here], rcv.at[a, c, me],
                        fwd_send.at[a], fwd_recv.at[a, c], seq,
                    ).start()

            @pl.when(step == 0)
            def _():
                for a in range(2):
                    pltpu.make_async_copy(
                        nrm.at[a, me, here], rcv.at[a, c, me], fwd_recv.at[a, c]
                    ).start()

            return carry

        lax.fori_loop(0, SEQ, one, 0)

    send_values(0)

    @pl.when(me == 0)
    def _():
        for step in range(1, dp_size):
            pl.semaphore_signal(
                ready, inc=1, device_id={"dp": lax.rem(dp + step, dp_size)}, device_id_type=MESH
            )
        pl.semaphore_wait(ready, dp_size - 1)
        for step in range(1, SEQ):
            pl.semaphore_signal(
                everyone, inc=1, device_id={"seq": lax.rem(me + step, SEQ)}, device_id_type=MESH
            )

    @pl.when(me > 0)
    def _():
        pl.semaphore_wait(everyone, 1)

    for copy in gain_loads:
        copy.wait()
    for step in range(1, dp_size):
        remote_dp(
            gsend, gbuf.at[dp], gain_send, gain_recv, lax.rem(dp + step, dp_size)
        ).start()
    pltpu.make_async_copy(gsend, gbuf.at[dp], gain_recv).start()
    send_values(1)

    row_ids = lax.broadcasted_iota(jnp.int32, mask.shape, 0)
    col_ids = lax.broadcasted_iota(jnp.int32, mask.shape, 1)
    allowed = (lax.rem(row_ids, GROUP) == lax.rem(col_ids, GROUP)) & (col_ids <= row_ids)
    mask[...] = jnp.where(allowed, 0.0, NEGATIVE)
    acc[...] = jnp.zeros_like(acc)

    pltpu.make_async_copy(gbuf, gbuf, gain_recv).wait()
    for d in range(dp_size):
        for a in range(2):
            gain[a, d * local_heads : (d + 1) * local_heads] = gbuf[
                d, a * pad : a * pad + local_heads
            ]
    for copy in raw_loads:
        copy.wait()

    send_normalized(0)
    send_normalized(1)
    for c in range(2, CHUNKS):
        send_values(c)
        send_normalized(c)

    def contract(left, right, dims):
        return lax.dot_general(left, right, (dims, ((), ())), preferred_element_type=jnp.float32)

    def attention(c):
        for a in range(4):
            pltpu.make_async_copy(rcv.at[a, c], rcv.at[a, c], fwd_recv.at[a, c]).wait()

        def block(b, carry):
            here = pl.ds(pl.multiple_of(b * GROUP, GROUP), GROUP)
            wide = SEQ * GROUP
            query, key, value, grad = (
                rcv[a, c, :, here, :].reshape(wide, HDIM) for a in range(4)
            )
            scores = contract(query, key, ((1,), (1,))) * scaling + mask[...]
            expo = jnp.exp(scores - jnp.max(scores, axis=-1, keepdims=True))
            probability = expo / jnp.sum(expo, axis=-1, keepdims=True)
            prob_low = probability.astype(jnp.bfloat16)
            prob_grad = contract(grad, value, ((1,), (1,)))
            row_dots = jnp.sum(prob_low.astype(jnp.float32) * prob_grad, axis=-1, keepdims=True)
            score_low = (probability * (prob_grad - row_dots)).astype(jnp.bfloat16)
            results = (
                contract(score_low, key, ((1,), (0,))) * scaling,
                contract(score_low, query, ((0,), (0,))) * scaling,
                contract(prob_low, grad, ((0,), (0,))),
            )
            for a, result in enumerate(results):
                stg[a, c, :, here, :] = result.astype(jnp.bfloat16).reshape(SEQ, GROUP, HDIM)
            return carry

        lax.fori_loop(0, part // GROUP, block, 0)

    def send_steps(c):
        def one(step, carry):
            seq = peer_of(me, step)
            for a in range(2):
                remote(
                    stg.at[a, c, seq], ret.at[a, c, me], ret_send.at[a], ret_recv.at[a, c], seq
                ).start()
            return carry

        lax.fori_loop(1, SEQ, one, 0)
        for a in range(2):
            pltpu.make_async_copy(stg.at[a, c, me], ret.at[a, c, me], ret_recv.at[a, c]).start()

    def send_value_grads(c):
        here = pl.ds(c * part, part)

        def one(step, carry):
            seq = peer_of(me, step)
            remote(stg.at[2, c, seq], ov.at[me, here], val_send, val_recv, seq).start()
            return carry

        lax.fori_loop(1, SEQ, one, 0)
        pltpu.make_async_copy(stg.at[2, c, me], ov.at[me, here], val_recv).start()

    def norm_back(c):
        here = pl.ds(c * part, part)
        for a in range(2):
            pltpu.make_async_copy(ret.at[a, c], ret.at[a, c], ret_recv.at[a, c]).wait()

        def one(seq, carry):
            for a in range(2):
                hat, inverse = normalized(a, seq, here)
                step = ret[a, c, seq].astype(jnp.float32)
                gained = by_head(step, gain[a])
                mean = jnp.mean(gained * hat, axis=-1, keepdims=True)
                held[a][seq, here] = (inverse * (gained - hat * mean)).astype(jnp.bfloat16)
                acc[a] += jnp.sum((step * hat).reshape(part // HEADS, HEADS, HDIM), axis=0)
            return carry

        lax.fori_loop(0, SEQ, one, 0)

    lots = (0, CHUNKS // 4, CHUNKS // 2, 3 * CHUNKS // 4, CHUNKS)

    def send_lot(lot):
        for c in range(lots[lot], lots[lot + 1]):
            send_value_grads(c)

    for c in range(CHUNKS):
        attention(c)
        send_steps(c)
    send_lot(0)
    for c in range(CHUNKS):
        norm_back(c)

    rsend[...] = jnp.zeros_like(rsend)
    for d in range(dp_size):
        for a in range(2):
            rsend[d, a * pad : a * pad + local_heads] = acc[
                a, d * local_heads : (d + 1) * local_heads
            ]
    for step in range(1, dp_size):
        other = lax.rem(dp + step, dp_size)
        remote_dp(rsend.at[other], rbuf.at[dp], rs_send, rs_recv, other).start()
    pltpu.make_async_copy(rsend.at[dp], rbuf.at[dp], rs_recv).start()
    send_lot(1)
    pltpu.make_async_copy(rbuf, rbuf, rs_recv).wait()
    asend[...] = jnp.sum(rbuf[...], axis=0).reshape(asend.shape)
    for step in range(1, SEQ):
        seq = lax.rem(me + step, SEQ)
        remote(asend.at[seq], abuf.at[me], row_send, row_recv, seq).start()
    pltpu.make_async_copy(asend.at[me], abuf.at[me], row_recv).start()
    send_lot(2)
    pltpu.make_async_copy(abuf, abuf, row_recv).wait()
    row[...] = jnp.sum(abuf[...], axis=0)
    for step in range(1, SEQ):
        seq = lax.rem(me + step, SEQ)
        remote(row, bbuf.at[me], ag_send, ag_recv, seq).start()
    pltpu.make_async_copy(row, bbuf.at[me], ag_recv).start()
    send_lot(3)
    pltpu.make_async_copy(bbuf, bbuf, ag_recv).wait()
    total_gain[...] = bbuf[...].reshape(total_gain.shape)

    others = pl.ds(0, SEQ - 1)
    pltpu.make_async_copy(ov, ov, val_recv).wait()
    for a in range(4):
        pltpu.make_async_copy(oq.at[others], oq.at[others], fwd_send.at[a]).wait()
    for a in range(2):
        pltpu.make_async_copy(oq.at[others], oq.at[others], ret_send.at[a]).wait()
    pltpu.make_async_copy(oq.at[others], oq.at[others], val_send).wait()
    if dp_size > 1:
        most = pl.ds(0, dp_size - 1)
        pltpu.make_async_copy(gbuf.at[most], gbuf.at[most], gain_send).wait()
        pltpu.make_async_copy(rbuf.at[most], rbuf.at[most], rs_send).wait()
    pltpu.make_async_copy(abuf.at[others], abuf.at[others], row_send).wait()
    pltpu.make_async_copy(bbuf.at[others], bbuf.at[others], ag_send).wait()


def write_out(local_heads, oq, ok, ov, total_gain, *refs):
    outs, sems = refs[:5], refs[5]
    pad = total_gain.shape[0] // 2
    quarter = SEQ // 4
    copies = [
        pltpu.make_async_copy(source.at[here], out.at[here], sems.at[i, n])
        for n, here in enumerate(pl.ds(q * quarter, quarter) for q in range(4))
        for i, (source, out) in enumerate(zip((oq, ok, ov), outs))
    ]
    for a in range(2):
        source = total_gain.at[pl.ds(a * pad, local_heads)]
        copies.append(pltpu.make_async_copy(source, outs[3 + a], sems.at[3, a]))
    for copy in copies:
        copy.start()
    for copy in copies:
        copy.wait()


def body(dp_size, queries, key_proj, value_proj, out_grad, query_gain, key_gain):
    shape = queries.shape
    rows = shape[2] * HEADS // SEQ
    part = rows // CHUNKS
    local_heads = query_gain.shape[0]
    pad = SEQ // 2
    flat = [v.reshape(SEQ, rows, HDIM) for v in (queries, key_proj, value_proj, out_grad)]
    low, wide = jnp.bfloat16, jnp.float32
    gap = ((0, pad - local_heads), (0, 0))
    gains = jnp.concatenate([jnp.pad(query_gain, gap), jnp.pad(key_gain, gap)], axis=0)
    anywhere = pl.BlockSpec(memory_space=pl.ANY)
    vmem = pl.BlockSpec(memory_space=pltpu.VMEM)
    dma = pltpu.SemaphoreType.DMA
    big = jax.ShapeDtypeStruct((SEQ, rows, HDIM), low)
    small = jax.ShapeDtypeStruct((local_heads, HDIM), wide)
    results = pl.pallas_call(
        functools.partial(kernel, dp_size),
        out_shape=(big, big, big, jax.ShapeDtypeStruct((2 * pad, HDIM), wide)),
        in_specs=[anywhere] * 5,
        out_specs=(vmem,) * 4,
        scratch_shapes=[
            pltpu.VMEM((2, SEQ, rows, HDIM), low),
            pltpu.VMEM((4, CHUNKS, SEQ, part, HDIM), low),
            pltpu.VMEM((3, CHUNKS, SEQ, part, HDIM), low),
            pltpu.VMEM((2, CHUNKS, SEQ, part, HDIM), low),
            pltpu.VMEM((SEQ * GROUP, SEQ * GROUP), wide),
            pltpu.VMEM((2 * pad, HDIM), wide),
            pltpu.VMEM((dp_size, 2 * pad, HDIM), wide),
            pltpu.VMEM((2, HEADS, HDIM), wide),
            pltpu.VMEM((2, HEADS, HDIM), wide),
            pltpu.VMEM((dp_size, 2 * pad, HDIM), wide),
            pltpu.VMEM((dp_size, 2 * pad, HDIM), wide),
            pltpu.VMEM((SEQ, 1, HDIM), wide),
            pltpu.VMEM((SEQ, 1, HDIM), wide),
            pltpu.VMEM((1, HDIM), wide),
            pltpu.VMEM((SEQ, 1, HDIM), wide),
            dma((2,)),
            dma,
            dma((4,)),
            dma((4, CHUNKS)),
            dma((2,)),
            dma((2, CHUNKS)),
            dma,
            dma,
            dma,
            dma,
            dma,
            dma,
            dma,
            dma,
            dma,
            dma,
            pltpu.SemaphoreType.REGULAR,
            pltpu.SemaphoreType.REGULAR,
        ],
        compiler_params=pltpu.CompilerParams(
            collective_id=0, has_side_effects=True, vmem_limit_bytes=44 * 2**20
        ),
        name="temporal_attention_backward",
    )(*flat, gains)
    query_grad, key_grad, value_grad, query_total, key_total = pl.pallas_call(
        functools.partial(write_out, local_heads),
        out_shape=(big, big, big, small, small),
        in_specs=[vmem] * 4,
        out_specs=(anywhere,) * 5,
        scratch_shapes=[dma((4, 4))],
        compiler_params=pltpu.CompilerParams(vmem_limit_bytes=2**20),
        name="write_out",
    )(*results)
    return (
        query_grad.reshape(shape),
        key_grad.reshape(shape),
        value_grad.reshape(shape),
        query_total,
        key_total,
    )


def solution(mesh):
    blocks = P("dp", "seq", None, None, None)
    gains = P("dp", None)
    return jax.shard_map(
        functools.partial(body, mesh.shape["dp"]),
        mesh=mesh,
        in_specs=(blocks, blocks, blocks, blocks, gains, gains),
        out_specs=(blocks, blocks, blocks, gains, gains),
        check_vma=False,
    )
```

```python
import functools
import math

import jax
import jax.numpy as jnp
from jax import lax
from jax.experimental import pallas as pl
from jax.experimental.pallas import tpu as pltpu
from jax.sharding import PartitionSpec as P

EPSILON = 1e-06
HEADS = 40
HDIM = 128
SEQ = 16
CHUNKS = 8
GROUP = 16
MESH = pl.DeviceIdType.MESH
NEGATIVE = -1e30


def peer_of(me, step):
    step = lax.rem(step * 9, SEQ)
    x = lax.rem(lax.div(me, 8) + lax.div(step, 8), 2)
    z = lax.rem(lax.div(me, 2) + lax.div(step, 2), 4)
    core = lax.rem(me + step, 2)
    return x * 8 + z * 2 + core


def kernel(
    dp_size,
    q_hbm, k_hbm, v_hbm, g_hbm, gains_hbm,
    oq, ok, ov, total_gain,
    nrm, rcv, stg, ret, mask, gsend, gbuf, gain, acc, rsend, rbuf, asend, abuf, row, bbuf,
    raw_sem, load_sem, fwd_send, fwd_recv, ret_send, ret_recv, val_send, val_recv,
    gain_send, gain_recv, rs_send, rs_recv, row_send, row_recv, ag_send, ag_recv,
    ready, everyone,
):
    me = lax.axis_index("seq")
    dp = lax.axis_index("dp")
    rows = q_hbm.shape[1]
    part = rows // CHUNKS
    y, xh = lax.div(dp, 2), lax.rem(dp, 2)
    sides = dp_size // 2
    partner = 2 * y + 1 - xh
    local_heads = HEADS // dp_size
    pad = SEQ // 2
    scaling = 1.0 / math.sqrt(HDIM)

    def remote(src, dst, send, recv, seq):
        return pltpu.make_async_remote_copy(
            src_ref=src, dst_ref=dst, send_sem=send, recv_sem=recv,
            device_id={"seq": seq}, device_id_type=MESH,
        )

    def remote_dp(src, dst, send, recv, other):
        return pltpu.make_async_remote_copy(
            src_ref=src, dst_ref=dst, send_sem=send, recv_sem=recv,
            device_id={"dp": other}, device_id_type=MESH,
        )

    barrier = pltpu.get_barrier_semaphore()
    for step in range(1, SEQ):
        pl.semaphore_signal(
            barrier, inc=1, device_id={"seq": lax.rem(me + step, SEQ)}, device_id_type=MESH
        )

    @pl.when(me == 0)
    def _():
        for step in range(1, dp_size):
            pl.semaphore_signal(
                barrier, inc=1, device_id={"dp": lax.rem(dp + step, dp_size)}, device_id_type=MESH
            )

    held = (oq, ok)
    gain_loads = [pltpu.make_async_copy(gains_hbm, gsend, load_sem)]
    raw_loads = [
        pltpu.make_async_copy(source, held[a], raw_sem.at[a])
        for a, source in enumerate((q_hbm, k_hbm))
    ]
    for copy in gain_loads + raw_loads:
        copy.start()

    @pl.when(me == 0)
    def _():
        pl.semaphore_wait(barrier, SEQ - 1 + dp_size - 1)

    @pl.when(me > 0)
    def _():
        pl.semaphore_wait(barrier, SEQ - 1)

    def send_values(c):
        here = pl.ds(c * part, part)

        def one(step, carry):
            seq = peer_of(me, step)
            for a, source in ((2, v_hbm), (3, g_hbm)):
                remote(
                    source.at[seq, here], rcv.at[a, c, me], fwd_send.at[a], fwd_recv.at[a, c], seq
                ).start()
            return carry

        lax.fori_loop(1, SEQ, one, 0)
        for a, source in ((2, v_hbm), (3, g_hbm)):
            pltpu.make_async_copy(source.at[me, here], rcv.at[a, c, me], fwd_recv.at[a, c]).start()

    def normalized(a, seq, here):
        wide = held[a][seq, here].astype(jnp.float32)
        inverse = lax.rsqrt(jnp.mean(wide * wide, axis=-1, keepdims=True) + EPSILON)
        return wide * inverse, inverse

    def by_head(tile, factor):
        split = tile.reshape(part // HEADS, HEADS, HDIM)
        return (split * factor[None]).reshape(part, HDIM)

    def send_normalized(c):
        here = pl.ds(c * part, part)

        def one(step, carry):
            seq = peer_of(me, step)
            for a in range(2):
                hat, _ = normalized(a, seq, here)
                nrm[a, seq, here] = by_head(hat, gain[a]).astype(jnp.bfloat16)

            @pl.when(step > 0)
            def _():
                for a in range(2):
                    remote(
                        nrm.at[a, seq, here], rcv.at[a, c, me],
                        fwd_send.at[a], fwd_recv.at[a, c], seq,
                    ).start()

            @pl.when(step == 0)
            def _():
                for a in range(2):
                    pltpu.make_async_copy(
                        nrm.at[a, me, here], rcv.at[a, c, me], fwd_recv.at[a, c]
                    ).start()

            return carry

        lax.fori_loop(0, SEQ, one, 0)

    send_values(0)
    send_values(1)

    @pl.when(me == 0)
    def _():
        for step in range(1, dp_size):
            pl.semaphore_signal(
                ready, inc=1, device_id={"dp": lax.rem(dp + step, dp_size)}, device_id_type=MESH
            )
        pl.semaphore_wait(ready, dp_size - 1)
        for step in range(1, SEQ):
            pl.semaphore_signal(
                everyone, inc=1, device_id={"seq": lax.rem(me + step, SEQ)}, device_id_type=MESH
            )

    @pl.when(me > 0)
    def _():
        pl.semaphore_wait(everyone, 1)

    for copy in gain_loads:
        copy.wait()
    remote_dp(gsend, gbuf.at[dp], gain_send.at[0], gain_recv.at[0], partner).start()
    pltpu.make_async_copy(gsend, gbuf.at[dp], gain_recv.at[0]).start()
    send_values(2)
    both = gbuf.at[pl.ds(2 * y, 2)]
    pltpu.make_async_copy(both, both, gain_recv.at[0]).wait()
    for step in range(1, sides):
        other = lax.rem(y + step, sides) * 2 + xh
        remote_dp(both, both, gain_send.at[1], gain_recv.at[1], other).start()
    for c in range(3, CHUNKS):
        send_values(c)

    row_ids = lax.broadcasted_iota(jnp.int32, mask.shape, 0)
    col_ids = lax.broadcasted_iota(jnp.int32, mask.shape, 1)
    allowed = (lax.rem(row_ids, GROUP) == lax.rem(col_ids, GROUP)) & (col_ids <= row_ids)
    mask[...] = jnp.where(allowed, 0.0, NEGATIVE)
    acc[...] = jnp.zeros_like(acc)

    rest = gbuf.at[pl.ds(0, dp_size - 2)]
    pltpu.make_async_copy(rest, rest, gain_recv.at[1]).wait()
    for d in range(dp_size):
        for a in range(2):
            gain[a, d * local_heads : (d + 1) * local_heads] = gbuf[
                d, a * pad : a * pad + local_heads
            ]
    for copy in raw_loads:
        copy.wait()

    for c in range(CHUNKS):
        send_normalized(c)

    def contract(left, right, dims):
        return lax.dot_general(left, right, (dims, ((), ())), preferred_element_type=jnp.float32)

    def attention(c):
        for a in range(4):
            pltpu.make_async_copy(rcv.at[a, c], rcv.at[a, c], fwd_recv.at[a, c]).wait()

        def block(b, carry):
            here = pl.ds(pl.multiple_of(b * GROUP, GROUP), GROUP)
            wide = SEQ * GROUP
            query, key, value, grad = (
                rcv[a, c, :, here, :].reshape(wide, HDIM) for a in range(4)
            )
            scores = contract(query, key, ((1,), (1,))) * scaling + mask[...]
            expo = jnp.exp(scores - jnp.max(scores, axis=-1, keepdims=True))
            probability = expo / jnp.sum(expo, axis=-1, keepdims=True)
            prob_low = probability.astype(jnp.bfloat16)
            prob_grad = contract(grad, value, ((1,), (1,)))
            row_dots = jnp.sum(prob_low.astype(jnp.float32) * prob_grad, axis=-1, keepdims=True)
            score_low = (probability * (prob_grad - row_dots)).astype(jnp.bfloat16)
            results = (
                contract(score_low, key, ((1,), (0,))) * scaling,
                contract(score_low, query, ((0,), (0,))) * scaling,
                contract(prob_low, grad, ((0,), (0,))),
            )
            for a, result in enumerate(results):
                stg[a, c, :, here, :] = result.astype(jnp.bfloat16).reshape(SEQ, GROUP, HDIM)
            return carry

        lax.fori_loop(0, part // GROUP, block, 0)

    def send_steps(c):
        def one(step, carry):
            seq = peer_of(me, step)
            for a in range(2):
                remote(
                    stg.at[a, c, seq], ret.at[a, c, me], ret_send.at[a], ret_recv.at[a, c], seq
                ).start()
            return carry

        lax.fori_loop(1, SEQ, one, 0)
        for a in range(2):
            pltpu.make_async_copy(stg.at[a, c, me], ret.at[a, c, me], ret_recv.at[a, c]).start()

    def send_value_grads(c):
        here = pl.ds(c * part, part)

        def one(step, carry):
            seq = peer_of(me, step)
            remote(stg.at[2, c, seq], ov.at[me, here], val_send, val_recv, seq).start()
            return carry

        lax.fori_loop(1, SEQ, one, 0)
        pltpu.make_async_copy(stg.at[2, c, me], ov.at[me, here], val_recv).start()

    def norm_back(c):
        here = pl.ds(c * part, part)
        for a in range(2):
            pltpu.make_async_copy(ret.at[a, c], ret.at[a, c], ret_recv.at[a, c]).wait()

        def one(seq, carry):
            for a in range(2):
                hat, inverse = normalized(a, seq, here)
                step = ret[a, c, seq].astype(jnp.float32)
                gained = by_head(step, gain[a])
                mean = jnp.mean(gained * hat, axis=-1, keepdims=True)
                held[a][seq, here] = (inverse * (gained - hat * mean)).astype(jnp.bfloat16)
                acc[a] += jnp.sum((step * hat).reshape(part // HEADS, HEADS, HDIM), axis=0)
            return carry

        lax.fori_loop(0, SEQ, one, 0)

    lots = (0, CHUNKS // 4, CHUNKS // 2, 3 * CHUNKS // 4, CHUNKS)

    def send_lot(lot):
        for c in range(lots[lot], lots[lot + 1]):
            send_value_grads(c)

    for c in range(CHUNKS):
        attention(c)
        send_steps(c)
    send_lot(0)
    for c in range(CHUNKS):
        norm_back(c)

    rsend[...] = jnp.zeros_like(rsend)
    for d in range(dp_size):
        for a in range(2):
            rsend[d, a * pad : a * pad + local_heads] = acc[
                a, d * local_heads : (d + 1) * local_heads
            ]
    for step in range(1, dp_size):
        other = lax.rem(dp + step, dp_size)
        remote_dp(rsend.at[other], rbuf.at[dp], rs_send, rs_recv, other).start()
    pltpu.make_async_copy(rsend.at[dp], rbuf.at[dp], rs_recv).start()
    send_lot(1)
    pltpu.make_async_copy(rbuf, rbuf, rs_recv).wait()
    asend[...] = jnp.sum(rbuf[...], axis=0).reshape(asend.shape)
    for step in range(1, SEQ):
        seq = lax.rem(me + step, SEQ)
        remote(asend.at[seq], abuf.at[me], row_send, row_recv, seq).start()
    pltpu.make_async_copy(asend.at[me], abuf.at[me], row_recv).start()
    send_lot(2)
    pltpu.make_async_copy(abuf, abuf, row_recv).wait()
    row[...] = jnp.sum(abuf[...], axis=0)
    for step in range(1, SEQ):
        seq = lax.rem(me + step, SEQ)
        remote(row, bbuf.at[me], ag_send, ag_recv, seq).start()
    pltpu.make_async_copy(row, bbuf.at[me], ag_recv).start()
    send_lot(3)
    pltpu.make_async_copy(bbuf, bbuf, ag_recv).wait()
    total_gain[...] = bbuf[...].reshape(total_gain.shape)

    others = pl.ds(0, SEQ - 1)
    pltpu.make_async_copy(ov, ov, val_recv).wait()
    for a in range(4):
        pltpu.make_async_copy(oq.at[others], oq.at[others], fwd_send.at[a]).wait()
    for a in range(2):
        pltpu.make_async_copy(oq.at[others], oq.at[others], ret_send.at[a]).wait()
    pltpu.make_async_copy(oq.at[others], oq.at[others], val_send).wait()
    pltpu.make_async_copy(gsend, gsend, gain_send.at[0]).wait()
    pltpu.make_async_copy(rest, rest, gain_send.at[1]).wait()
    most = rbuf.at[pl.ds(0, dp_size - 1)]
    pltpu.make_async_copy(most, most, rs_send).wait()
    pltpu.make_async_copy(abuf.at[others], abuf.at[others], row_send).wait()
    pltpu.make_async_copy(bbuf.at[others], bbuf.at[others], ag_send).wait()


def write_out(local_heads, oq, ok, ov, total_gain, *refs):
    outs, sems = refs[:5], refs[5]
    pad = total_gain.shape[0] // 2
    quarter = SEQ // 4
    copies = [
        pltpu.make_async_copy(source.at[here], out.at[here], sems.at[i, n])
        for n, here in enumerate(pl.ds(q * quarter, quarter) for q in range(4))
        for i, (source, out) in enumerate(zip((oq, ok, ov), outs))
    ]
    for a in range(2):
        source = total_gain.at[pl.ds(a * pad, local_heads)]
        copies.append(pltpu.make_async_copy(source, outs[3 + a], sems.at[3, a]))
    for copy in copies:
        copy.start()
    for copy in copies:
        copy.wait()


def body(dp_size, queries, key_proj, value_proj, out_grad, query_gain, key_gain):
    shape = queries.shape
    rows = shape[2] * HEADS // SEQ
    part = rows // CHUNKS
    local_heads = query_gain.shape[0]
    pad = SEQ // 2
    flat = [v.reshape(SEQ, rows, HDIM) for v in (queries, key_proj, value_proj, out_grad)]
    low, wide = jnp.bfloat16, jnp.float32
    gap = ((0, pad - local_heads), (0, 0))
    gains = jnp.concatenate([jnp.pad(query_gain, gap), jnp.pad(key_gain, gap)], axis=0)
    anywhere = pl.BlockSpec(memory_space=pl.ANY)
    vmem = pl.BlockSpec(memory_space=pltpu.VMEM)
    dma = pltpu.SemaphoreType.DMA
    big = jax.ShapeDtypeStruct((SEQ, rows, HDIM), low)
    small = jax.ShapeDtypeStruct((local_heads, HDIM), wide)
    results = pl.pallas_call(
        functools.partial(kernel, dp_size),
        out_shape=(big, big, big, jax.ShapeDtypeStruct((2 * pad, HDIM), wide)),
        in_specs=[anywhere] * 5,
        out_specs=(vmem,) * 4,
        scratch_shapes=[
            pltpu.VMEM((2, SEQ, rows, HDIM), low),
            pltpu.VMEM((4, CHUNKS, SEQ, part, HDIM), low),
            pltpu.VMEM((3, CHUNKS, SEQ, part, HDIM), low),
            pltpu.VMEM((2, CHUNKS, SEQ, part, HDIM), low),
            pltpu.VMEM((SEQ * GROUP, SEQ * GROUP), wide),
            pltpu.VMEM((2 * pad, HDIM), wide),
            pltpu.VMEM((dp_size, 2 * pad, HDIM), wide),
            pltpu.VMEM((2, HEADS, HDIM), wide),
            pltpu.VMEM((2, HEADS, HDIM), wide),
            pltpu.VMEM((dp_size, 2 * pad, HDIM), wide),
            pltpu.VMEM((dp_size, 2 * pad, HDIM), wide),
            pltpu.VMEM((SEQ, 1, HDIM), wide),
            pltpu.VMEM((SEQ, 1, HDIM), wide),
            pltpu.VMEM((1, HDIM), wide),
            pltpu.VMEM((SEQ, 1, HDIM), wide),
            dma((2,)),
            dma,
            dma((4,)),
            dma((4, CHUNKS)),
            dma((2,)),
            dma((2, CHUNKS)),
            dma,
            dma,
            dma((2,)),
            dma((2,)),
            dma,
            dma,
            dma,
            dma,
            dma,
            dma,
            pltpu.SemaphoreType.REGULAR,
            pltpu.SemaphoreType.REGULAR,
        ],
        compiler_params=pltpu.CompilerParams(
            collective_id=0, has_side_effects=True, vmem_limit_bytes=44 * 2**20
        ),
        name="temporal_attention_backward",
    )(*flat, gains)
    query_grad, key_grad, value_grad, query_total, key_total = pl.pallas_call(
        functools.partial(write_out, local_heads),
        out_shape=(big, big, big, small, small),
        in_specs=[vmem] * 4,
        out_specs=(anywhere,) * 5,
        scratch_shapes=[dma((4, 4))],
        compiler_params=pltpu.CompilerParams(vmem_limit_bytes=2**20),
        name="write_out",
    )(*results)
    return (
        query_grad.reshape(shape),
        key_grad.reshape(shape),
        value_grad.reshape(shape),
        query_total,
        key_total,
    )


def solution(mesh):
    blocks = P("dp", "seq", None, None, None)
    gains = P("dp", None)
    return jax.shard_map(
        functools.partial(body, mesh.shape["dp"]),
        mesh=mesh,
        in_specs=(blocks, blocks, blocks, blocks, gains, gains),
        out_specs=(blocks, blocks, blocks, gains, gains),
        check_vma=False,
    )
```

```python
import functools
import math

import jax
import jax.numpy as jnp
from jax import lax
from jax.experimental import pallas as pl
from jax.experimental.pallas import tpu as pltpu
from jax.sharding import PartitionSpec as P

EPSILON = 1e-06
HEADS = 40
HDIM = 128
SEQ = 16
CHUNKS = 8
GROUP = 16
MESH = pl.DeviceIdType.MESH
NEGATIVE = -1e30


def peer_of(me, step):
    step = lax.rem(step * 7, SEQ)
    x = lax.rem(lax.div(me, 8) + lax.div(step, 8), 2)
    z = lax.rem(lax.div(me, 2) + lax.div(step, 2), 4)
    core = lax.rem(me + step, 2)
    return x * 8 + z * 2 + core


def kernel(
    dp_size,
    q_hbm, k_hbm, v_hbm, g_hbm, gains_hbm,
    oq, ok, ov, total_gain,
    nrm, rcv, stg, ret, mask, gsend, gbuf, gain, acc, rsend, rbuf, asend, abuf, row, swapped, final, bbuf,
    raw_sem, load_sem, fwd_send, fwd_recv, ret_send, ret_recv, val_send, val_recv,
    gain_send, gain_recv, rs_send, rs_recv, row_send, row_recv, ag_send, ag_recv,
    ready, everyone, swap_send, swap_recv,
):
    me = lax.axis_index("seq")
    dp = lax.axis_index("dp")
    rows = q_hbm.shape[1]
    part = rows // CHUNKS
    y, xh = lax.div(dp, 2), lax.rem(dp, 2)
    sides = dp_size // 2
    partner = 2 * y + 1 - xh
    local_heads = HEADS // dp_size
    pad = SEQ // 2
    scaling = 1.0 / math.sqrt(HDIM)

    def remote(src, dst, send, recv, seq):
        return pltpu.make_async_remote_copy(
            src_ref=src, dst_ref=dst, send_sem=send, recv_sem=recv,
            device_id={"seq": seq}, device_id_type=MESH,
        )

    def remote_dp(src, dst, send, recv, other):
        return pltpu.make_async_remote_copy(
            src_ref=src, dst_ref=dst, send_sem=send, recv_sem=recv,
            device_id={"dp": other}, device_id_type=MESH,
        )

    barrier = pltpu.get_barrier_semaphore()
    for step in range(1, SEQ):
        pl.semaphore_signal(
            barrier, inc=1, device_id={"seq": lax.rem(me + step, SEQ)}, device_id_type=MESH
        )

    @pl.when(me == 0)
    def _():
        for step in range(1, dp_size):
            pl.semaphore_signal(
                barrier, inc=1, device_id={"dp": lax.rem(dp + step, dp_size)}, device_id_type=MESH
            )

    held = (oq, ok)
    gain_loads = [pltpu.make_async_copy(gains_hbm, gsend, load_sem)]
    raw_loads = [
        pltpu.make_async_copy(source, held[a], raw_sem.at[a])
        for a, source in enumerate((q_hbm, k_hbm))
    ]
    for copy in gain_loads + raw_loads:
        copy.start()

    @pl.when(me == 0)
    def _():
        pl.semaphore_wait(barrier, SEQ - 1 + dp_size - 1)

    @pl.when(me > 0)
    def _():
        pl.semaphore_wait(barrier, SEQ - 1)

    def send_values(c):
        here = pl.ds(c * part, part)

        def one(step, carry):
            seq = peer_of(me, step)
            for a, source in ((2, v_hbm), (3, g_hbm)):
                remote(
                    source.at[seq, here], rcv.at[a, c, me], fwd_send.at[a], fwd_recv.at[a, c], seq
                ).start()
            return carry

        lax.fori_loop(1, SEQ, one, 0)
        for a, source in ((2, v_hbm), (3, g_hbm)):
            pltpu.make_async_copy(source.at[me, here], rcv.at[a, c, me], fwd_recv.at[a, c]).start()

    def normalized(a, seq, here):
        wide = held[a][seq, here].astype(jnp.float32)
        inverse = lax.rsqrt(jnp.mean(wide * wide, axis=-1, keepdims=True) + EPSILON)
        return wide * inverse, inverse

    def by_head(tile, factor):
        split = tile.reshape(part // HEADS, HEADS, HDIM)
        return (split * factor[None]).reshape(part, HDIM)

    def send_normalized(c):
        here = pl.ds(c * part, part)

        def one(step, carry):
            seq = peer_of(me, step)
            for a in range(2):
                hat, _ = normalized(a, seq, here)
                nrm[a, seq, here] = by_head(hat, gain[a]).astype(jnp.bfloat16)

            @pl.when(step > 0)
            def _():
                for a in range(2):
                    remote(
                        nrm.at[a, seq, here], rcv.at[a, c, me],
                        fwd_send.at[a], fwd_recv.at[a, c], seq,
                    ).start()

            @pl.when(step == 0)
            def _():
                for a in range(2):
                    pltpu.make_async_copy(
                        nrm.at[a, me, here], rcv.at[a, c, me], fwd_recv.at[a, c]
                    ).start()

            return carry

        lax.fori_loop(0, SEQ, one, 0)

    send_values(0)
    send_values(1)

    @pl.when(me == 0)
    def _():
        for step in range(1, dp_size):
            pl.semaphore_signal(
                ready, inc=1, device_id={"dp": lax.rem(dp + step, dp_size)}, device_id_type=MESH
            )
        pl.semaphore_wait(ready, dp_size - 1)
        for step in range(1, SEQ):
            pl.semaphore_signal(
                everyone, inc=1, device_id={"seq": lax.rem(me + step, SEQ)}, device_id_type=MESH
            )

    @pl.when(me > 0)
    def _():
        pl.semaphore_wait(everyone, 1)

    for copy in gain_loads:
        copy.wait()
    remote_dp(gsend, gbuf.at[dp], gain_send.at[0], gain_recv.at[0], partner).start()
    pltpu.make_async_copy(gsend, gbuf.at[dp], gain_recv.at[0]).start()
    send_values(2)
    both = gbuf.at[pl.ds(2 * y, 2)]
    pltpu.make_async_copy(both, both, gain_recv.at[0]).wait()
    for step in range(1, sides):
        other = lax.rem(y + step, sides) * 2 + xh
        remote_dp(both, both, gain_send.at[1], gain_recv.at[1], other).start()
    for c in range(3, CHUNKS):
        send_values(c)

    row_ids = lax.broadcasted_iota(jnp.int32, mask.shape, 0)
    col_ids = lax.broadcasted_iota(jnp.int32, mask.shape, 1)
    allowed = (lax.rem(row_ids, GROUP) == lax.rem(col_ids, GROUP)) & (col_ids <= row_ids)
    mask[...] = jnp.where(allowed, 0.0, NEGATIVE)
    acc[...] = jnp.zeros_like(acc)

    rest = gbuf.at[pl.ds(0, dp_size - 2)]
    pltpu.make_async_copy(rest, rest, gain_recv.at[1]).wait()
    for d in range(dp_size):
        for a in range(2):
            gain[a, d * local_heads : (d + 1) * local_heads] = gbuf[
                d, a * pad : a * pad + local_heads
            ]
    for copy in raw_loads:
        copy.wait()

    for c in range(CHUNKS):
        send_normalized(c)

    def contract(left, right, dims):
        return lax.dot_general(left, right, (dims, ((), ())), preferred_element_type=jnp.float32)

    def attention(c):
        for a in range(4):
            pltpu.make_async_copy(rcv.at[a, c], rcv.at[a, c], fwd_recv.at[a, c]).wait()

        def block(b, carry):
            here = pl.ds(pl.multiple_of(b * GROUP, GROUP), GROUP)
            wide = SEQ * GROUP
            query, key, value, grad = (
                rcv[a, c, :, here, :].reshape(wide, HDIM) for a in range(4)
            )
            scores = contract(query, key, ((1,), (1,))) * scaling + mask[...]
            expo = jnp.exp(scores - jnp.max(scores, axis=-1, keepdims=True))
            probability = expo / jnp.sum(expo, axis=-1, keepdims=True)
            prob_low = probability.astype(jnp.bfloat16)
            prob_grad = contract(grad, value, ((1,), (1,)))
            row_dots = jnp.sum(prob_low.astype(jnp.float32) * prob_grad, axis=-1, keepdims=True)
            score_low = (probability * (prob_grad - row_dots)).astype(jnp.bfloat16)
            results = (
                contract(score_low, key, ((1,), (0,))) * scaling,
                contract(score_low, query, ((0,), (0,))) * scaling,
                contract(prob_low, grad, ((0,), (0,))),
            )
            for a, result in enumerate(results):
                stg[a, c, :, here, :] = result.astype(jnp.bfloat16).reshape(SEQ, GROUP, HDIM)
            return carry

        lax.fori_loop(0, part // GROUP, block, 0)

    def send_steps(c):
        def one(step, carry):
            seq = peer_of(me, step)
            for a in range(2):
                remote(
                    stg.at[a, c, seq], ret.at[a, c, me], ret_send.at[a], ret_recv.at[a, c], seq
                ).start()
            return carry

        lax.fori_loop(1, SEQ, one, 0)
        for a in range(2):
            pltpu.make_async_copy(stg.at[a, c, me], ret.at[a, c, me], ret_recv.at[a, c]).start()

    def send_value_grads(c):
        here = pl.ds(c * part, part)

        def one(step, carry):
            seq = peer_of(me, step)
            remote(stg.at[2, c, seq], ov.at[me, here], val_send, val_recv, seq).start()
            return carry

        lax.fori_loop(1, SEQ, one, 0)
        pltpu.make_async_copy(stg.at[2, c, me], ov.at[me, here], val_recv).start()

    def norm_back(c):
        here = pl.ds(c * part, part)
        for a in range(2):
            pltpu.make_async_copy(ret.at[a, c], ret.at[a, c], ret_recv.at[a, c]).wait()

        def one(seq, carry):
            for a in range(2):
                hat, inverse = normalized(a, seq, here)
                step = ret[a, c, seq].astype(jnp.float32)
                gained = by_head(step, gain[a])
                mean = jnp.mean(gained * hat, axis=-1, keepdims=True)
                held[a][seq, here] = (inverse * (gained - hat * mean)).astype(jnp.bfloat16)
                acc[a] += jnp.sum((step * hat).reshape(part // HEADS, HEADS, HDIM), axis=0)
            return carry

        lax.fori_loop(0, SEQ, one, 0)

    lots = (0, 2, 4, 6, 7, CHUNKS)

    def send_lot(lot):
        for c in range(lots[lot], lots[lot + 1]):
            send_value_grads(c)

    for c in range(CHUNKS):
        attention(c)
        send_steps(c)
    send_lot(0)
    for c in range(CHUNKS):
        norm_back(c)

    rsend[...] = jnp.zeros_like(rsend)
    for d in range(dp_size):
        for a in range(2):
            rsend[d, a * pad : a * pad + local_heads] = acc[
                a, d * local_heads : (d + 1) * local_heads
            ]
    for step in range(1, sides):
        other = lax.rem(y + step, sides)
        remote_dp(
            rsend.at[pl.ds(2 * other, 2)], rbuf.at[y], rs_send, rs_recv, 2 * other + xh
        ).start()
    pltpu.make_async_copy(rsend.at[pl.ds(2 * y, 2)], rbuf.at[y], rs_recv).start()
    send_lot(1)
    pltpu.make_async_copy(rbuf, rbuf, rs_recv).wait()
    asend[...] = jnp.sum(rbuf[...], axis=0).reshape(asend.shape)
    for step in range(1, SEQ):
        seq = lax.rem(me + step, SEQ)
        remote(asend.at[:, seq], abuf.at[me], row_send, row_recv, seq).start()
    pltpu.make_async_copy(asend.at[:, me], abuf.at[me], row_recv).start()
    send_lot(2)
    pltpu.make_async_copy(abuf, abuf, row_recv).wait()
    row[...] = jnp.sum(abuf[...], axis=0)
    swap = remote_dp(row.at[1 - xh], swapped, swap_send, swap_recv, partner)
    swap.start()
    send_lot(3)
    swap.wait()
    final[...] = row[xh] + swapped[...]
    for step in range(1, SEQ):
        seq = lax.rem(me + step, SEQ)
        remote(final, bbuf.at[me], ag_send, ag_recv, seq).start()
    pltpu.make_async_copy(final, bbuf.at[me], ag_recv).start()
    send_lot(4)
    pltpu.make_async_copy(bbuf, bbuf, ag_recv).wait()
    total_gain[...] = bbuf[...].reshape(total_gain.shape)

    others = pl.ds(0, SEQ - 1)
    pltpu.make_async_copy(ov, ov, val_recv).wait()
    for a in range(4):
        pltpu.make_async_copy(oq.at[others], oq.at[others], fwd_send.at[a]).wait()
    for a in range(2):
        pltpu.make_async_copy(oq.at[others], oq.at[others], ret_send.at[a]).wait()
    pltpu.make_async_copy(oq.at[others], oq.at[others], val_send).wait()
    pltpu.make_async_copy(gsend, gsend, gain_send.at[0]).wait()
    pltpu.make_async_copy(rest, rest, gain_send.at[1]).wait()
    most = rbuf.at[pl.ds(0, sides - 1)]
    pltpu.make_async_copy(most, most, rs_send).wait()
    pltpu.make_async_copy(abuf.at[others], abuf.at[others], row_send).wait()
    pltpu.make_async_copy(bbuf.at[others], bbuf.at[others], ag_send).wait()


def write_out(local_heads, oq, ok, ov, total_gain, *refs):
    outs, sems = refs[:5], refs[5]
    pad = total_gain.shape[0] // 2
    quarter = SEQ // 4
    copies = [
        pltpu.make_async_copy(source.at[here], out.at[here], sems.at[i, n])
        for n, here in enumerate(pl.ds(q * quarter, quarter) for q in range(4))
        for i, (source, out) in enumerate(zip((oq, ok, ov), outs))
    ]
    for a in range(2):
        source = total_gain.at[pl.ds(a * pad, local_heads)]
        copies.append(pltpu.make_async_copy(source, outs[3 + a], sems.at[3, a]))
    for copy in copies:
        copy.start()
    for copy in copies:
        copy.wait()


def body(dp_size, queries, key_proj, value_proj, out_grad, query_gain, key_gain):
    shape = queries.shape
    rows = shape[2] * HEADS // SEQ
    part = rows // CHUNKS
    local_heads = query_gain.shape[0]
    pad = SEQ // 2
    flat = [v.reshape(SEQ, rows, HDIM) for v in (queries, key_proj, value_proj, out_grad)]
    low, wide = jnp.bfloat16, jnp.float32
    gap = ((0, pad - local_heads), (0, 0))
    gains = jnp.concatenate([jnp.pad(query_gain, gap), jnp.pad(key_gain, gap)], axis=0)
    anywhere = pl.BlockSpec(memory_space=pl.ANY)
    vmem = pl.BlockSpec(memory_space=pltpu.VMEM)
    dma = pltpu.SemaphoreType.DMA
    big = jax.ShapeDtypeStruct((SEQ, rows, HDIM), low)
    small = jax.ShapeDtypeStruct((local_heads, HDIM), wide)
    results = pl.pallas_call(
        functools.partial(kernel, dp_size),
        out_shape=(big, big, big, jax.ShapeDtypeStruct((2 * pad, HDIM), wide)),
        in_specs=[anywhere] * 5,
        out_specs=(vmem,) * 4,
        scratch_shapes=[
            pltpu.VMEM((2, SEQ, rows, HDIM), low),
            pltpu.VMEM((4, CHUNKS, SEQ, part, HDIM), low),
            pltpu.VMEM((3, CHUNKS, SEQ, part, HDIM), low),
            pltpu.VMEM((2, CHUNKS, SEQ, part, HDIM), low),
            pltpu.VMEM((SEQ * GROUP, SEQ * GROUP), wide),
            pltpu.VMEM((2 * pad, HDIM), wide),
            pltpu.VMEM((dp_size, 2 * pad, HDIM), wide),
            pltpu.VMEM((2, HEADS, HDIM), wide),
            pltpu.VMEM((2, HEADS, HDIM), wide),
            pltpu.VMEM((dp_size, 2 * pad, HDIM), wide),
            pltpu.VMEM((dp_size // 2, 2, 2 * pad, HDIM), wide),
            pltpu.VMEM((2, SEQ, 1, HDIM), wide),
            pltpu.VMEM((SEQ, 2, 1, HDIM), wide),
            pltpu.VMEM((2, 1, HDIM), wide),
            pltpu.VMEM((1, HDIM), wide),
            pltpu.VMEM((1, HDIM), wide),
            pltpu.VMEM((SEQ, 1, HDIM), wide),
            dma((2,)),
            dma,
            dma((4,)),
            dma((4, CHUNKS)),
            dma((2,)),
            dma((2, CHUNKS)),
            dma,
            dma,
            dma((2,)),
            dma((2,)),
            dma,
            dma,
            dma,
            dma,
            dma,
            dma,
            pltpu.SemaphoreType.REGULAR,
            pltpu.SemaphoreType.REGULAR,
            dma,
            dma,
        ],
        compiler_params=pltpu.CompilerParams(
            collective_id=0, has_side_effects=True, vmem_limit_bytes=44 * 2**20
        ),
        name="temporal_attention_backward",
    )(*flat, gains)
    query_grad, key_grad, value_grad, query_total, key_total = pl.pallas_call(
        functools.partial(write_out, local_heads),
        out_shape=(big, big, big, small, small),
        in_specs=[vmem] * 4,
        out_specs=(anywhere,) * 5,
        scratch_shapes=[dma((4, 4))],
        compiler_params=pltpu.CompilerParams(vmem_limit_bytes=2**20),
        name="write_out",
    )(*results)
    return (
        query_grad.reshape(shape),
        key_grad.reshape(shape),
        value_grad.reshape(shape),
        query_total,
        key_total,
    )


def solution(mesh):
    blocks = P("dp", "seq", None, None, None)
    gains = P("dp", None)
    return jax.shard_map(
        functools.partial(body, mesh.shape["dp"]),
        mesh=mesh,
        in_specs=(blocks, blocks, blocks, blocks, gains, gains),
        out_specs=(blocks, blocks, blocks, gains, gains),
        check_vma=False,
    )
```

```python
import functools
import math

import jax
import jax.numpy as jnp
from jax import lax
from jax.experimental import pallas as pl
from jax.experimental.pallas import tpu as pltpu
from jax.sharding import PartitionSpec as P

EPSILON = 1e-06
HEADS = 40
HDIM = 128
SEQ = 16
CHUNKS = 8
GROUP = 16
MESH = pl.DeviceIdType.MESH
NEGATIVE = -1e30


def peer_of(me, step):
    step = lax.rem(step * 13, SEQ)
    x = lax.rem(lax.div(me, 8) + lax.div(step, 8), 2)
    z = lax.rem(lax.div(me, 2) + lax.div(step, 2), 4)
    core = lax.rem(me + step, 2)
    return x * 8 + z * 2 + core


def kernel(
    dp_size,
    q_hbm, k_hbm, v_hbm, g_hbm, gains_hbm,
    oq, ok, ov, total_gain,
    nrm, rcv, stg, ret, mask, gsend, gbuf, gain, acc, rsend, rbuf, asend, abuf, row, swapped, final, bbuf,
    raw_sem, load_sem, fwd_send, fwd_recv, ret_send, ret_recv, val_send, val_recv,
    gain_send, gain_recv, rs_send, rs_recv, row_send, row_recv, ag_send, ag_recv,
    ready, everyone, swap_send, swap_recv,
):
    me = lax.axis_index("seq")
    dp = lax.axis_index("dp")
    rows = q_hbm.shape[1]
    part = rows // CHUNKS
    y, xh = lax.div(dp, 2), lax.rem(dp, 2)
    sides = dp_size // 2
    partner = 2 * y + 1 - xh
    local_heads = HEADS // dp_size
    pad = SEQ // 2
    scaling = 1.0 / math.sqrt(HDIM)

    def remote(src, dst, send, recv, seq):
        return pltpu.make_async_remote_copy(
            src_ref=src, dst_ref=dst, send_sem=send, recv_sem=recv,
            device_id={"seq": seq}, device_id_type=MESH,
        )

    def remote_dp(src, dst, send, recv, other):
        return pltpu.make_async_remote_copy(
            src_ref=src, dst_ref=dst, send_sem=send, recv_sem=recv,
            device_id={"dp": other}, device_id_type=MESH,
        )

    barrier = pltpu.get_barrier_semaphore()
    for step in range(1, SEQ):
        pl.semaphore_signal(
            barrier, inc=1, device_id={"seq": lax.rem(me + step, SEQ)}, device_id_type=MESH
        )

    @pl.when(me == 0)
    def _():
        for step in range(1, dp_size):
            pl.semaphore_signal(
                barrier, inc=1, device_id={"dp": lax.rem(dp + step, dp_size)}, device_id_type=MESH
            )

    held = (oq, ok)
    gain_loads = [pltpu.make_async_copy(gains_hbm, gsend, load_sem)]
    raw_loads = [
        pltpu.make_async_copy(source, held[a], raw_sem.at[a])
        for a, source in enumerate((q_hbm, k_hbm))
    ]
    for copy in gain_loads + raw_loads:
        copy.start()

    @pl.when(me == 0)
    def _():
        pl.semaphore_wait(barrier, SEQ - 1 + dp_size - 1)

    @pl.when(me > 0)
    def _():
        pl.semaphore_wait(barrier, SEQ - 1)

    def send_values(c):
        here = pl.ds(c * part, part)

        def one(step, carry):
            seq = peer_of(me, step)
            for a, source in ((2, v_hbm), (3, g_hbm)):
                remote(
                    source.at[seq, here], rcv.at[a, c, me], fwd_send.at[a], fwd_recv.at[a, c], seq
                ).start()
            return carry

        lax.fori_loop(1, SEQ, one, 0)
        for a, source in ((2, v_hbm), (3, g_hbm)):
            pltpu.make_async_copy(source.at[me, here], rcv.at[a, c, me], fwd_recv.at[a, c]).start()

    def normalized(a, seq, here):
        wide = held[a][seq, here].astype(jnp.float32)
        inverse = lax.rsqrt(jnp.mean(wide * wide, axis=-1, keepdims=True) + EPSILON)
        return wide * inverse, inverse

    def by_head(tile, factor):
        split = tile.reshape(part // HEADS, HEADS, HDIM)
        return (split * factor[None]).reshape(part, HDIM)

    def send_normalized(c):
        here = pl.ds(c * part, part)

        def one(step, carry):
            seq = peer_of(me, step)
            for a in range(2):
                hat, _ = normalized(a, seq, here)
                nrm[a, seq, here] = by_head(hat, gain[a]).astype(jnp.bfloat16)

            @pl.when(step > 0)
            def _():
                for a in range(2):
                    remote(
                        nrm.at[a, seq, here], rcv.at[a, c, me],
                        fwd_send.at[a], fwd_recv.at[a, c], seq,
                    ).start()

            @pl.when(step == 0)
            def _():
                for a in range(2):
                    pltpu.make_async_copy(
                        nrm.at[a, me, here], rcv.at[a, c, me], fwd_recv.at[a, c]
                    ).start()

            return carry

        lax.fori_loop(0, SEQ, one, 0)

    send_values(0)
    send_values(1)

    @pl.when(me == 0)
    def _():
        for step in range(1, dp_size):
            pl.semaphore_signal(
                ready, inc=1, device_id={"dp": lax.rem(dp + step, dp_size)}, device_id_type=MESH
            )
        pl.semaphore_wait(ready, dp_size - 1)
        for step in range(1, SEQ):
            pl.semaphore_signal(
                everyone, inc=1, device_id={"seq": lax.rem(me + step, SEQ)}, device_id_type=MESH
            )

    @pl.when(me > 0)
    def _():
        pl.semaphore_wait(everyone, 1)

    for copy in gain_loads:
        copy.wait()
    remote_dp(gsend, gbuf.at[dp], gain_send.at[0], gain_recv.at[0], partner).start()
    pltpu.make_async_copy(gsend, gbuf.at[dp], gain_recv.at[0]).start()
    send_values(2)
    both = gbuf.at[pl.ds(2 * y, 2)]
    pltpu.make_async_copy(both, both, gain_recv.at[0]).wait()
    for step in range(1, sides):
        other = lax.rem(y + step, sides) * 2 + xh
        remote_dp(both, both, gain_send.at[1], gain_recv.at[1], other).start()
    for c in range(3, CHUNKS):
        send_values(c)

    row_ids = lax.broadcasted_iota(jnp.int32, mask.shape, 0)
    col_ids = lax.broadcasted_iota(jnp.int32, mask.shape, 1)
    allowed = (lax.rem(row_ids, GROUP) == lax.rem(col_ids, GROUP)) & (col_ids <= row_ids)
    mask[...] = jnp.where(allowed, 0.0, NEGATIVE)
    acc[...] = jnp.zeros_like(acc)

    rest = gbuf.at[pl.ds(0, dp_size - 2)]
    pltpu.make_async_copy(rest, rest, gain_recv.at[1]).wait()
    for d in range(dp_size):
        for a in range(2):
            gain[a, d * local_heads : (d + 1) * local_heads] = gbuf[
                d, a * pad : a * pad + local_heads
            ]
    for copy in raw_loads:
        copy.wait()

    for c in range(CHUNKS):
        send_normalized(c)

    def contract(left, right, dims):
        return lax.dot_general(left, right, (dims, ((), ())), preferred_element_type=jnp.float32)

    def attention(c):
        for a in range(4):
            pltpu.make_async_copy(rcv.at[a, c], rcv.at[a, c], fwd_recv.at[a, c]).wait()

        def block(b, carry):
            here = pl.ds(pl.multiple_of(b * GROUP, GROUP), GROUP)
            wide = SEQ * GROUP
            query, key, value, grad = (
                rcv[a, c, :, here, :].reshape(wide, HDIM) for a in range(4)
            )
            scores = contract(query, key, ((1,), (1,))) * scaling + mask[...]
            expo = jnp.exp(scores - jnp.max(scores, axis=-1, keepdims=True))
            probability = expo / jnp.sum(expo, axis=-1, keepdims=True)
            prob_low = probability.astype(jnp.bfloat16)
            prob_grad = contract(grad, value, ((1,), (1,)))
            row_dots = jnp.sum(prob_low.astype(jnp.float32) * prob_grad, axis=-1, keepdims=True)
            score_low = (probability * (prob_grad - row_dots)).astype(jnp.bfloat16)
            results = (
                contract(score_low, key, ((1,), (0,))) * scaling,
                contract(score_low, query, ((0,), (0,))) * scaling,
                contract(prob_low, grad, ((0,), (0,))),
            )
            for a, result in enumerate(results):
                stg[a, c, :, here, :] = result.astype(jnp.bfloat16).reshape(SEQ, GROUP, HDIM)
            return carry

        lax.fori_loop(0, part // GROUP, block, 0)

    def send_steps(c):
        def one(step, carry):
            seq = peer_of(me, step)
            for a in range(2):
                remote(
                    stg.at[a, c, seq], ret.at[a, c, me], ret_send.at[a], ret_recv.at[a, c], seq
                ).start()
            return carry

        lax.fori_loop(1, SEQ, one, 0)
        for a in range(2):
            pltpu.make_async_copy(stg.at[a, c, me], ret.at[a, c, me], ret_recv.at[a, c]).start()

    def send_value_grads(c):
        here = pl.ds(c * part, part)

        def one(step, carry):
            seq = peer_of(me, step)
            remote(stg.at[2, c, seq], ov.at[me, here], val_send, val_recv, seq).start()
            return carry

        lax.fori_loop(1, SEQ, one, 0)
        pltpu.make_async_copy(stg.at[2, c, me], ov.at[me, here], val_recv).start()

    def norm_back(c):
        here = pl.ds(c * part, part)
        for a in range(2):
            pltpu.make_async_copy(ret.at[a, c], ret.at[a, c], ret_recv.at[a, c]).wait()

        def one(seq, carry):
            for a in range(2):
                hat, inverse = normalized(a, seq, here)
                step = ret[a, c, seq].astype(jnp.float32)
                gained = by_head(step, gain[a])
                mean = jnp.mean(gained * hat, axis=-1, keepdims=True)
                held[a][seq, here] = (inverse * (gained - hat * mean)).astype(jnp.bfloat16)
                acc[a] += jnp.sum((step * hat).reshape(part // HEADS, HEADS, HDIM), axis=0)
            return carry

        lax.fori_loop(0, SEQ, one, 0)

    lots = (0, 2, 4, 6, 7, CHUNKS)

    def send_lot(lot):
        for c in range(lots[lot], lots[lot + 1]):
            send_value_grads(c)

    for c in range(CHUNKS):
        attention(c)
        send_steps(c)
    send_lot(0)
    for c in range(CHUNKS):
        norm_back(c)

    rsend[...] = jnp.zeros_like(rsend)
    for d in range(dp_size):
        for a in range(2):
            rsend[d, a * pad : a * pad + local_heads] = acc[
                a, d * local_heads : (d + 1) * local_heads
            ]
    for step in range(1, sides):
        other = lax.rem(y + step, sides)
        remote_dp(
            rsend.at[pl.ds(2 * other, 2)], rbuf.at[y], rs_send, rs_recv, 2 * other + xh
        ).start()
    pltpu.make_async_copy(rsend.at[pl.ds(2 * y, 2)], rbuf.at[y], rs_recv).start()
    send_lot(1)
    pltpu.make_async_copy(rbuf, rbuf, rs_recv).wait()
    asend[...] = jnp.sum(rbuf[...], axis=0).reshape(asend.shape)
    for step in range(1, SEQ):
        seq = lax.rem(me + step, SEQ)
        remote(asend.at[:, seq], abuf.at[me], row_send, row_recv, seq).start()
    pltpu.make_async_copy(asend.at[:, me], abuf.at[me], row_recv).start()
    send_lot(2)
    pltpu.make_async_copy(abuf, abuf, row_recv).wait()
    row[...] = jnp.sum(abuf[...], axis=0)
    swap = remote_dp(row.at[1 - xh], swapped, swap_send, swap_recv, partner)
    swap.start()
    send_lot(3)
    swap.wait()
    final[...] = row[xh] + swapped[...]
    for step in range(1, SEQ):
        seq = lax.rem(me + step, SEQ)
        remote(final, bbuf.at[me], ag_send, ag_recv, seq).start()
    pltpu.make_async_copy(final, bbuf.at[me], ag_recv).start()
    send_lot(4)
    pltpu.make_async_copy(bbuf, bbuf, ag_recv).wait()
    total_gain[...] = bbuf[...].reshape(total_gain.shape)

    others = pl.ds(0, SEQ - 1)
    pltpu.make_async_copy(ov, ov, val_recv).wait()
    for a in range(4):
        pltpu.make_async_copy(oq.at[others], oq.at[others], fwd_send.at[a]).wait()
    for a in range(2):
        pltpu.make_async_copy(oq.at[others], oq.at[others], ret_send.at[a]).wait()
    pltpu.make_async_copy(oq.at[others], oq.at[others], val_send).wait()
    pltpu.make_async_copy(gsend, gsend, gain_send.at[0]).wait()
    pltpu.make_async_copy(rest, rest, gain_send.at[1]).wait()
    most = rbuf.at[pl.ds(0, sides - 1)]
    pltpu.make_async_copy(most, most, rs_send).wait()
    pltpu.make_async_copy(abuf.at[others], abuf.at[others], row_send).wait()
    pltpu.make_async_copy(bbuf.at[others], bbuf.at[others], ag_send).wait()


def write_out(local_heads, oq, ok, ov, total_gain, *refs):
    outs, sems = refs[:5], refs[5]
    pad = total_gain.shape[0] // 2
    quarter = SEQ // 4
    copies = [
        pltpu.make_async_copy(source.at[here], out.at[here], sems.at[i, n])
        for n, here in enumerate(pl.ds(q * quarter, quarter) for q in range(4))
        for i, (source, out) in enumerate(zip((oq, ok, ov), outs))
    ]
    for a in range(2):
        source = total_gain.at[pl.ds(a * pad, local_heads)]
        copies.append(pltpu.make_async_copy(source, outs[3 + a], sems.at[3, a]))
    for copy in copies:
        copy.start()
    for copy in copies:
        copy.wait()


def body(dp_size, queries, key_proj, value_proj, out_grad, query_gain, key_gain):
    shape = queries.shape
    rows = shape[2] * HEADS // SEQ
    part = rows // CHUNKS
    local_heads = query_gain.shape[0]
    pad = SEQ // 2
    flat = [v.reshape(SEQ, rows, HDIM) for v in (queries, key_proj, value_proj, out_grad)]
    low, wide = jnp.bfloat16, jnp.float32
    gap = ((0, pad - local_heads), (0, 0))
    gains = jnp.concatenate([jnp.pad(query_gain, gap), jnp.pad(key_gain, gap)], axis=0)
    anywhere = pl.BlockSpec(memory_space=pl.ANY)
    vmem = pl.BlockSpec(memory_space=pltpu.VMEM)
    dma = pltpu.SemaphoreType.DMA
    big = jax.ShapeDtypeStruct((SEQ, rows, HDIM), low)
    small = jax.ShapeDtypeStruct((local_heads, HDIM), wide)
    results = pl.pallas_call(
        functools.partial(kernel, dp_size),
        out_shape=(big, big, big, jax.ShapeDtypeStruct((2 * pad, HDIM), wide)),
        in_specs=[anywhere] * 5,
        out_specs=(vmem,) * 4,
        scratch_shapes=[
            pltpu.VMEM((2, SEQ, rows, HDIM), low),
            pltpu.VMEM((4, CHUNKS, SEQ, part, HDIM), low),
            pltpu.VMEM((3, CHUNKS, SEQ, part, HDIM), low),
            pltpu.VMEM((2, CHUNKS, SEQ, part, HDIM), low),
            pltpu.VMEM((SEQ * GROUP, SEQ * GROUP), wide),
            pltpu.VMEM((2 * pad, HDIM), wide),
            pltpu.VMEM((dp_size, 2 * pad, HDIM), wide),
            pltpu.VMEM((2, HEADS, HDIM), wide),
            pltpu.VMEM((2, HEADS, HDIM), wide),
            pltpu.VMEM((dp_size, 2 * pad, HDIM), wide),
            pltpu.VMEM((dp_size // 2, 2, 2 * pad, HDIM), wide),
            pltpu.VMEM((2, SEQ, 1, HDIM), wide),
            pltpu.VMEM((SEQ, 2, 1, HDIM), wide),
            pltpu.VMEM((2, 1, HDIM), wide),
            pltpu.VMEM((1, HDIM), wide),
            pltpu.VMEM((1, HDIM), wide),
            pltpu.VMEM((SEQ, 1, HDIM), wide),
            dma((2,)),
            dma,
            dma((4,)),
            dma((4, CHUNKS)),
            dma((2,)),
            dma((2, CHUNKS)),
            dma,
            dma,
            dma((2,)),
            dma((2,)),
            dma,
            dma,
            dma,
            dma,
            dma,
            dma,
            pltpu.SemaphoreType.REGULAR,
            pltpu.SemaphoreType.REGULAR,
            dma,
            dma,
        ],
        compiler_params=pltpu.CompilerParams(
            collective_id=0, has_side_effects=True, vmem_limit_bytes=44 * 2**20
        ),
        name="temporal_attention_backward",
    )(*flat, gains)
    query_grad, key_grad, value_grad, query_total, key_total = pl.pallas_call(
        functools.partial(write_out, local_heads),
        out_shape=(big, big, big, small, small),
        in_specs=[vmem] * 4,
        out_specs=(anywhere,) * 5,
        scratch_shapes=[dma((4, 4))],
        compiler_params=pltpu.CompilerParams(vmem_limit_bytes=2**20),
        name="write_out",
    )(*results)
    return (
        query_grad.reshape(shape),
        key_grad.reshape(shape),
        value_grad.reshape(shape),
        query_total,
        key_total,
    )


def solution(mesh):
    blocks = P("dp", "seq", None, None, None)
    gains = P("dp", None)
    return jax.shard_map(
        functools.partial(body, mesh.shape["dp"]),
        mesh=mesh,
        in_specs=(blocks, blocks, blocks, blocks, gains, gains),
        out_specs=(blocks, blocks, blocks, gains, gains),
        check_vma=False,
    )
```

```python
import functools
import math

import jax
import jax.numpy as jnp
from jax import lax
from jax.experimental import pallas as pl
from jax.experimental.pallas import tpu as pltpu
from jax.sharding import PartitionSpec as P

EPSILON = 1e-06
HEADS = 40
HDIM = 128
SEQ = 16
CHUNKS = 8
GROUP = 16
MESH = pl.DeviceIdType.MESH
NEGATIVE = -1e30


def peer_of(me, step):
    step = lax.rem(step * 13, SEQ)
    x = lax.rem(lax.div(me, 8) + lax.div(step, 8), 2)
    z = lax.rem(lax.div(me, 2) + lax.div(step, 2), 4)
    core = lax.rem(me + step, 2)
    return x * 8 + z * 2 + core


def kernel(
    dp_size,
    q_hbm, k_hbm, v_hbm, g_hbm, gains_hbm,
    oq, ok, ov, total_gain,
    nrm, rcv, stg, ret, mask, gsend, gbuf, gain, acc, rsend, rbuf, asend, abuf, row, swapped, final, bbuf,
    raw_sem, load_sem, fwd_send, fwd_recv, ret_send, ret_recv, val_send, val_recv,
    gain_send, gain_recv, rs_send, rs_recv, row_send, row_recv, ag_send, ag_recv,
    ready, everyone, swap_send, swap_recv,
):
    me = lax.axis_index("seq")
    dp = lax.axis_index("dp")
    rows = q_hbm.shape[1]
    part = rows // CHUNKS
    y, xh = lax.div(dp, 2), lax.rem(dp, 2)
    sides = dp_size // 2
    partner = 2 * y + 1 - xh
    local_heads = HEADS // dp_size
    pad = SEQ // 2
    scaling = 1.0 / math.sqrt(HDIM)

    def remote(src, dst, send, recv, seq):
        return pltpu.make_async_remote_copy(
            src_ref=src, dst_ref=dst, send_sem=send, recv_sem=recv,
            device_id={"seq": seq}, device_id_type=MESH,
        )

    def remote_dp(src, dst, send, recv, other):
        return pltpu.make_async_remote_copy(
            src_ref=src, dst_ref=dst, send_sem=send, recv_sem=recv,
            device_id={"dp": other}, device_id_type=MESH,
        )

    barrier = pltpu.get_barrier_semaphore()
    for step in range(1, SEQ):
        pl.semaphore_signal(
            barrier, inc=1, device_id={"seq": lax.rem(me + step, SEQ)}, device_id_type=MESH
        )

    @pl.when(me == 0)
    def _():
        for step in range(1, dp_size):
            pl.semaphore_signal(
                barrier, inc=1, device_id={"dp": lax.rem(dp + step, dp_size)}, device_id_type=MESH
            )

    held = (oq, ok)
    gain_loads = [pltpu.make_async_copy(gains_hbm, gsend, load_sem)]
    raw_loads = [
        pltpu.make_async_copy(source, held[a], raw_sem.at[a])
        for a, source in enumerate((q_hbm, k_hbm))
    ]
    for copy in gain_loads + raw_loads:
        copy.start()

    @pl.when(me == 0)
    def _():
        pl.semaphore_wait(barrier, SEQ - 1 + dp_size - 1)

    @pl.when(me > 0)
    def _():
        pl.semaphore_wait(barrier, SEQ - 1)

    def send_values(c):
        here = pl.ds(c * part, part)

        def one(step, carry):
            seq = peer_of(me, step)
            for a, source in ((2, v_hbm), (3, g_hbm)):
                remote(
                    source.at[seq, here], rcv.at[a, c, me], fwd_send.at[a], fwd_recv.at[a, c], seq
                ).start()
            return carry

        lax.fori_loop(1, SEQ, one, 0)
        for a, source in ((2, v_hbm), (3, g_hbm)):
            pltpu.make_async_copy(source.at[me, here], rcv.at[a, c, me], fwd_recv.at[a, c]).start()

    def normalized(a, seq, here):
        wide = held[a][seq, here].astype(jnp.float32)
        inverse = lax.rsqrt(jnp.mean(wide * wide, axis=-1, keepdims=True) + EPSILON)
        return wide * inverse, inverse

    def by_head(tile, factor):
        split = tile.reshape(part // HEADS, HEADS, HDIM)
        return (split * factor[None]).reshape(part, HDIM)

    def send_normalized(c):
        here = pl.ds(c * part, part)

        def one(step, carry):
            seq = peer_of(me, step)
            for a in range(2):
                hat, _ = normalized(a, seq, here)
                nrm[a, seq, here] = by_head(hat, gain[a]).astype(jnp.bfloat16)

            @pl.when(step > 0)
            def _():
                for a in range(2):
                    remote(
                        nrm.at[a, seq, here], rcv.at[a, c, me],
                        fwd_send.at[a], fwd_recv.at[a, c], seq,
                    ).start()

            @pl.when(step == 0)
            def _():
                for a in range(2):
                    pltpu.make_async_copy(
                        nrm.at[a, me, here], rcv.at[a, c, me], fwd_recv.at[a, c]
                    ).start()

            return carry

        lax.fori_loop(0, SEQ, one, 0)

    send_values(0)
    send_values(1)

    @pl.when(me == 0)
    def _():
        for step in range(1, dp_size):
            pl.semaphore_signal(
                ready, inc=1, device_id={"dp": lax.rem(dp + step, dp_size)}, device_id_type=MESH
            )
        pl.semaphore_wait(ready, dp_size - 1)
        for step in range(1, SEQ):
            pl.semaphore_signal(
                everyone, inc=1, device_id={"seq": lax.rem(me + step, SEQ)}, device_id_type=MESH
            )

    @pl.when(me > 0)
    def _():
        pl.semaphore_wait(everyone, 1)

    for copy in gain_loads:
        copy.wait()
    remote_dp(gsend, gbuf.at[dp], gain_send.at[0], gain_recv.at[0], partner).start()
    pltpu.make_async_copy(gsend, gbuf.at[dp], gain_recv.at[0]).start()
    send_values(2)
    both = gbuf.at[pl.ds(2 * y, 2)]
    pltpu.make_async_copy(both, both, gain_recv.at[0]).wait()
    for step in range(1, sides):
        other = lax.rem(y + step, sides) * 2 + xh
        remote_dp(both, both, gain_send.at[1], gain_recv.at[1], other).start()
    for c in range(3, CHUNKS):
        send_values(c)

    row_ids = lax.broadcasted_iota(jnp.int32, mask.shape, 0)
    col_ids = lax.broadcasted_iota(jnp.int32, mask.shape, 1)
    allowed = (lax.rem(row_ids, GROUP) == lax.rem(col_ids, GROUP)) & (col_ids <= row_ids)
    mask[...] = jnp.where(allowed, 0.0, NEGATIVE)
    acc[...] = jnp.zeros_like(acc)

    rest = gbuf.at[pl.ds(0, dp_size - 2)]
    pltpu.make_async_copy(rest, rest, gain_recv.at[1]).wait()
    for d in range(dp_size):
        for a in range(2):
            gain[a, d * local_heads : (d + 1) * local_heads] = gbuf[
                d, a * pad : a * pad + local_heads
            ]
    for copy in raw_loads:
        copy.wait()

    for c in range(CHUNKS):
        send_normalized(c)

    def contract(left, right, dims):
        return lax.dot_general(left, right, (dims, ((), ())), preferred_element_type=jnp.float32)

    def attention(c):
        for a in range(4):
            pltpu.make_async_copy(rcv.at[a, c], rcv.at[a, c], fwd_recv.at[a, c]).wait()

        def block(b, carry):
            here = pl.ds(pl.multiple_of(b * GROUP, GROUP), GROUP)
            wide = SEQ * GROUP
            query, key, value, grad = (
                rcv[a, c, :, here, :].reshape(wide, HDIM) for a in range(4)
            )
            scores = contract(query, key, ((1,), (1,))) * scaling + mask[...]
            expo = jnp.exp(scores - jnp.max(scores, axis=-1, keepdims=True))
            probability = expo / jnp.sum(expo, axis=-1, keepdims=True)
            prob_low = probability.astype(jnp.bfloat16)
            prob_grad = contract(grad, value, ((1,), (1,)))
            row_dots = jnp.sum(prob_low.astype(jnp.float32) * prob_grad, axis=-1, keepdims=True)
            score_low = (probability * (prob_grad - row_dots)).astype(jnp.bfloat16)
            results = (
                contract(score_low, key, ((1,), (0,))) * scaling,
                contract(score_low, query, ((0,), (0,))) * scaling,
                contract(prob_low, grad, ((0,), (0,))),
            )
            for a, result in enumerate(results):
                stg[a, c, :, here, :] = result.astype(jnp.bfloat16).reshape(SEQ, GROUP, HDIM)
            return carry

        lax.fori_loop(0, part // GROUP, block, 0)

    def send_steps(c):
        def one(step, carry):
            seq = peer_of(me, step)
            for a in range(2):
                remote(
                    stg.at[a, c, seq], ret.at[a, c, me], ret_send.at[a], ret_recv.at[a, c], seq
                ).start()
            return carry

        lax.fori_loop(1, SEQ, one, 0)
        for a in range(2):
            pltpu.make_async_copy(stg.at[a, c, me], ret.at[a, c, me], ret_recv.at[a, c]).start()

    def send_value_grads(c):
        here = pl.ds(c * part, part)

        def one(step, carry):
            seq = peer_of(me, step)
            remote(stg.at[2, c, seq], ov.at[me, here], val_send, val_recv, seq).start()
            return carry

        lax.fori_loop(1, SEQ, one, 0)
        pltpu.make_async_copy(stg.at[2, c, me], ov.at[me, here], val_recv).start()

    def norm_back(c):
        here = pl.ds(c * part, part)
        for a in range(2):
            pltpu.make_async_copy(ret.at[a, c], ret.at[a, c], ret_recv.at[a, c]).wait()

        def one(seq, carry):
            for a in range(2):
                hat, inverse = normalized(a, seq, here)
                step = ret[a, c, seq].astype(jnp.float32)
                gained = by_head(step, gain[a])
                mean = jnp.mean(gained * hat, axis=-1, keepdims=True)
                held[a][seq, here] = (inverse * (gained - hat * mean)).astype(jnp.bfloat16)
                acc[a] += jnp.sum((step * hat).reshape(part // HEADS, HEADS, HDIM), axis=0)
            return carry

        lax.fori_loop(0, SEQ, one, 0, unroll=4)

    lots = (0, 2, 4, 6, 7, CHUNKS)

    def send_lot(lot):
        for c in range(lots[lot], lots[lot + 1]):
            send_value_grads(c)

    for c in range(CHUNKS):
        attention(c)
        send_steps(c)
    send_lot(0)
    for c in range(CHUNKS):
        norm_back(c)

    rsend[...] = jnp.zeros_like(rsend)
    for d in range(dp_size):
        for a in range(2):
            rsend[d, a * pad : a * pad + local_heads] = acc[
                a, d * local_heads : (d + 1) * local_heads
            ]
    for step in range(1, sides):
        other = lax.rem(y + step, sides)
        remote_dp(
            rsend.at[pl.ds(2 * other, 2)], rbuf.at[y], rs_send, rs_recv, 2 * other + xh
        ).start()
    pltpu.make_async_copy(rsend.at[pl.ds(2 * y, 2)], rbuf.at[y], rs_recv).start()
    send_lot(1)
    pltpu.make_async_copy(rbuf, rbuf, rs_recv).wait()
    asend[...] = jnp.sum(rbuf[...], axis=0).reshape(asend.shape)
    for step in range(1, SEQ):
        seq = lax.rem(me + step, SEQ)
        remote(asend.at[:, seq], abuf.at[me], row_send, row_recv, seq).start()
    pltpu.make_async_copy(asend.at[:, me], abuf.at[me], row_recv).start()
    send_lot(2)
    pltpu.make_async_copy(abuf, abuf, row_recv).wait()
    row[...] = jnp.sum(abuf[...], axis=0)
    swap = remote_dp(row.at[1 - xh], swapped, swap_send, swap_recv, partner)
    swap.start()
    send_lot(3)
    swap.wait()
    final[...] = row[xh] + swapped[...]
    for step in range(1, SEQ):
        seq = lax.rem(me + step, SEQ)
        remote(final, bbuf.at[me], ag_send, ag_recv, seq).start()
    pltpu.make_async_copy(final, bbuf.at[me], ag_recv).start()
    send_lot(4)
    pltpu.make_async_copy(bbuf, bbuf, ag_recv).wait()
    total_gain[...] = bbuf[...].reshape(total_gain.shape)

    others = pl.ds(0, SEQ - 1)
    pltpu.make_async_copy(ov, ov, val_recv).wait()
    for a in range(4):
        pltpu.make_async_copy(oq.at[others], oq.at[others], fwd_send.at[a]).wait()
    for a in range(2):
        pltpu.make_async_copy(oq.at[others], oq.at[others], ret_send.at[a]).wait()
    pltpu.make_async_copy(oq.at[others], oq.at[others], val_send).wait()
    pltpu.make_async_copy(gsend, gsend, gain_send.at[0]).wait()
    pltpu.make_async_copy(rest, rest, gain_send.at[1]).wait()
    most = rbuf.at[pl.ds(0, sides - 1)]
    pltpu.make_async_copy(most, most, rs_send).wait()
    pltpu.make_async_copy(abuf.at[others], abuf.at[others], row_send).wait()
    pltpu.make_async_copy(bbuf.at[others], bbuf.at[others], ag_send).wait()


def write_out(local_heads, oq, ok, ov, total_gain, *refs):
    outs, sems = refs[:5], refs[5]
    pad = total_gain.shape[0] // 2
    quarter = SEQ // 4
    copies = [
        pltpu.make_async_copy(source.at[here], out.at[here], sems.at[i, n])
        for n, here in enumerate(pl.ds(q * quarter, quarter) for q in range(4))
        for i, (source, out) in enumerate(zip((oq, ok, ov), outs))
    ]
    for a in range(2):
        source = total_gain.at[pl.ds(a * pad, local_heads)]
        copies.append(pltpu.make_async_copy(source, outs[3 + a], sems.at[3, a]))
    for copy in copies:
        copy.start()
    for copy in copies:
        copy.wait()


def body(dp_size, queries, key_proj, value_proj, out_grad, query_gain, key_gain):
    shape = queries.shape
    rows = shape[2] * HEADS // SEQ
    part = rows // CHUNKS
    local_heads = query_gain.shape[0]
    pad = SEQ // 2
    flat = [v.reshape(SEQ, rows, HDIM) for v in (queries, key_proj, value_proj, out_grad)]
    low, wide = jnp.bfloat16, jnp.float32
    gap = ((0, pad - local_heads), (0, 0))
    gains = jnp.concatenate([jnp.pad(query_gain, gap), jnp.pad(key_gain, gap)], axis=0)
    anywhere = pl.BlockSpec(memory_space=pl.ANY)
    vmem = pl.BlockSpec(memory_space=pltpu.VMEM)
    dma = pltpu.SemaphoreType.DMA
    big = jax.ShapeDtypeStruct((SEQ, rows, HDIM), low)
    small = jax.ShapeDtypeStruct((local_heads, HDIM), wide)
    results = pl.pallas_call(
        functools.partial(kernel, dp_size),
        out_shape=(big, big, big, jax.ShapeDtypeStruct((2 * pad, HDIM), wide)),
        in_specs=[anywhere] * 5,
        out_specs=(vmem,) * 4,
        scratch_shapes=[
            pltpu.VMEM((2, SEQ, rows, HDIM), low),
            pltpu.VMEM((4, CHUNKS, SEQ, part, HDIM), low),
            pltpu.VMEM((3, CHUNKS, SEQ, part, HDIM), low),
            pltpu.VMEM((2, CHUNKS, SEQ, part, HDIM), low),
            pltpu.VMEM((SEQ * GROUP, SEQ * GROUP), wide),
            pltpu.VMEM((2 * pad, HDIM), wide),
            pltpu.VMEM((dp_size, 2 * pad, HDIM), wide),
            pltpu.VMEM((2, HEADS, HDIM), wide),
            pltpu.VMEM((2, HEADS, HDIM), wide),
            pltpu.VMEM((dp_size, 2 * pad, HDIM), wide),
            pltpu.VMEM((dp_size // 2, 2, 2 * pad, HDIM), wide),
            pltpu.VMEM((2, SEQ, 1, HDIM), wide),
            pltpu.VMEM((SEQ, 2, 1, HDIM), wide),
            pltpu.VMEM((2, 1, HDIM), wide),
            pltpu.VMEM((1, HDIM), wide),
            pltpu.VMEM((1, HDIM), wide),
            pltpu.VMEM((SEQ, 1, HDIM), wide),
            dma((2,)),
            dma,
            dma((4,)),
            dma((4, CHUNKS)),
            dma((2,)),
            dma((2, CHUNKS)),
            dma,
            dma,
            dma((2,)),
            dma((2,)),
            dma,
            dma,
            dma,
            dma,
            dma,
            dma,
            pltpu.SemaphoreType.REGULAR,
            pltpu.SemaphoreType.REGULAR,
            dma,
            dma,
        ],
        compiler_params=pltpu.CompilerParams(
            collective_id=0, has_side_effects=True, vmem_limit_bytes=44 * 2**20
        ),
        name="temporal_attention_backward",
    )(*flat, gains)
    query_grad, key_grad, value_grad, query_total, key_total = pl.pallas_call(
        functools.partial(write_out, local_heads),
        out_shape=(big, big, big, small, small),
        in_specs=[vmem] * 4,
        out_specs=(anywhere,) * 5,
        scratch_shapes=[dma((4, 4))],
        compiler_params=pltpu.CompilerParams(vmem_limit_bytes=2**20),
        name="write_out",
    )(*results)
    return (
        query_grad.reshape(shape),
        key_grad.reshape(shape),
        value_grad.reshape(shape),
        query_total,
        key_total,
    )


def solution(mesh):
    blocks = P("dp", "seq", None, None, None)
    gains = P("dp", None)
    return jax.shard_map(
        functools.partial(body, mesh.shape["dp"]),
        mesh=mesh,
        in_specs=(blocks, blocks, blocks, blocks, gains, gains),
        out_specs=(blocks, blocks, blocks, gains, gains),
        check_vma=False,
    )
```
